256 devices in a mesh: seg: 16 (over z, core), term: 16 (over x, y).
Axes of the slice: x: 4, y: 4, z: 8, core: 2. Of those that a mesh axis runs over, the one named last changes fastest.
Arguments:
- wave_in: float32 [16, 16, 128, 128], P('seg')
- env_left: float32 [16, 64, 16, 128, 128], P('seg', 'term'), may hold values from -0.0625 to 0.0625
- env_right: float32 [16, 64, 16, 128, 128], P('seg', 'term'), may hold values from -0.5 to 0.5
- sector_charge: int32 [16, 2], replicated, may hold values from 0 to 3, as said below
- term_charge: int32 [64, 2], P('term'), may hold values from -1 to 1, as said below
- term_live: int32 [64], P('term'), may hold values from 0 to 1, as said below
- transfer: float32 [16, 16, 128, 128], P('seg'), may hold values from -0.15625 to 0.15625
Outputs:
- wave_out: float32 [16, 16, 128, 128], P('seg', 'term')
- new_env: float32 [16, 16, 128, 128], P('seg', 'term')
The draws below stay inside these ranges and needn't reach their ends.
Inputs may be any that keep to these rules, and one draw needn't show every extreme that they name: `sector_charge`: each of the 16 pairs (up, down) with both numbers in 0 .. 3 labels exactly one sector. `term_charge`: each term changes at most one of the two particle numbers, by one. `term_live`: in every draw some aligned group of 4 terms is all live.
All inputs are finite; a program needn't handle non-finite values.
Results may differ from the reference program's by a relative error of at most 0.0003.
Values sent between devices are 32-bit elements; how exact they have to be, the bound alone decides.
A program may use at most 128 MiB of HBM per device.

```python
import math
import jax
import jax.numpy as jnp
from jax import lax

BK = 128
CHARGES = 4
NS = 16
SLOTS = 4
TERMS = 64
NSEG = 16
ITERS = 3


def draw_sector_charge(key, part):
    key = jax.random.fold_in(key, 1)
    order = jax.random.permutation(key, NS)
    return jnp.stack([order // CHARGES, order % CHARGES], axis=1).astype(jnp.int32)


def draw_term_charge(key, part):
    key = jax.random.fold_in(key, 2)
    code = jax.random.randint(key, (TERMS,), 0, 5)
    up_change = (code == 1).astype(jnp.int32) - (code == 2).astype(jnp.int32)
    down_change = (code == 3).astype(jnp.int32) - (code == 4).astype(jnp.int32)
    return jnp.stack([up_change, down_change], axis=1).astype(jnp.int32)


def draw_term_live(key, part):
    key = jax.random.fold_in(key, 3)
    first, second = jax.random.split(key)
    flags = (jax.random.randint(first, (TERMS,), 0, 4) > 0).astype(jnp.int32)
    chosen = jax.random.randint(second, (), 0, TERMS // SLOTS)
    groups = jnp.arange(TERMS) // SLOTS
    return jnp.where(groups == chosen, 1, flags).astype(jnp.int32)


def draw_wave_in(key, part):
    key = jax.random.fold_in(key, 4)
    first, second, third = jax.random.split(key, 3)
    base = jax.random.normal(first, (NSEG, NS, BK, BK), jnp.float32)
    rows = jnp.exp(jax.random.uniform(second, (NSEG, NS, BK, 1), jnp.float32, 0.0, math.log(10.0)))
    cols = jnp.exp(jax.random.uniform(third, (NSEG, NS, 1, BK), jnp.float32, 0.0, math.log(10.0)))
    return (base * rows * cols).astype(jnp.float32)


def shard_levels(rng, shape, cuts, low, high):
    factor_of = 1.0
    for axis_at, shards_of in cuts:
        steps = jax.random.uniform(jax.random.fold_in(jax.random.fold_in(rng, 6), axis_at), (shards_of,), jnp.float32, low / len(cuts), high / len(cuts))
        factor_of = factor_of * jnp.repeat(jnp.exp(steps), shape[axis_at] // shards_of).reshape((-1,) + (1,) * (len(shape) - 1 - axis_at))
    return factor_of


def normal_values(key, dims, width, reach, shards=(), kind=jnp.bfloat16):
    drawn = width * jax.random.normal(key, dims, jnp.float32)
    if shards:
        drawn = drawn * shard_levels(key, dims, shards, -0.22, 0.18)
    return jnp.clip(drawn, -reach, reach).astype(kind)


def setup_inputs(seed: int = 0) -> dict:
    splits = jax.random.split(jax.random.key(seed), 8)
    return {
        "wave_in": draw_wave_in(jax.random.fold_in(splits[7], 71), 0),
        "env_left": normal_values(splits[1], (NSEG, TERMS, NS, BK, BK), (BK * TERMS) ** -0.5, 0.0625, ((0, 16), (1, 16)), jnp.float32),
        "env_right": normal_values(splits[2], (NSEG, TERMS, NS, BK, BK), BK ** -0.5, 0.5, ((0, 16), (1, 16)), jnp.float32),
        "sector_charge": draw_sector_charge(jax.random.fold_in(splits[7], 71), 0),
        "term_charge": draw_term_charge(jax.random.fold_in(splits[7], 71), 0),
        "term_live": draw_term_live(jax.random.fold_in(splits[7], 71), 0),
        "transfer": normal_values(splits[6], (NSEG, NS, BK, BK), (11 * BK) ** -0.5, 0.15625, ((0, 16),), jnp.float32),
    }


mean_eps = 1e-06
step_size = 0.5
HIGH = lax.Precision.HIGHEST

def source_tables(sector_charge, term_charge):
    target = sector_charge[None, :, :] - term_charge[:, None, :]
    match = jnp.all(target[:, :, None, :] == sector_charge[None, None, :, :], axis=3)
    return match.astype(jnp.float32)

def term_image(wave, table, left, right):
    moved = jnp.einsum('st,tbc->sbc', table, wave, precision=HIGH)
    inner = jnp.einsum('sab,sbc->sac', left, moved, precision=HIGH)
    return jnp.einsum('sac,sdc->sad', inner, right, precision=HIGH)

def normalize(wave):
    return wave * lax.rsqrt(jnp.mean(wave * wave) + mean_eps)

def one_bond(items):
    wave_in, env_l, env_r, tables, live = items
    wave = normalize(wave_in)
    image = jnp.zeros_like(wave)
    for step in range(ITERS):

        def add_term(total, xs):
            table, flag, left, right = xs
            return (total + flag * term_image(wave, table, left, right), None)
        image, unused = lax.scan(add_term, jnp.zeros_like(wave), (tables, live, env_l, env_r))
        theta = jnp.mean(wave * image)
        wave = normalize(wave - step_size * (image - theta * wave))
    energy = jnp.einsum('sab,sac->sbc', wave, image, precision=HIGH) / BK
    return (wave, energy)

def reference(wave_in, env_left, env_right, sector_charge, term_charge, term_live, transfer):
    tables = source_tables(sector_charge, term_charge)
    live = term_live.astype(jnp.float32)

    def per_bond(items):
        return one_bond((items[0], items[1], items[2], tables, live))
    wave_out, energy = lax.map(per_bond, (wave_in, env_left, env_right))
    step_map = jnp.eye(BK, dtype=jnp.float32)[None, None] + transfer
    previous = jnp.concatenate([jnp.zeros_like(energy[:1]), energy[:-1]], axis=0)

    def carry_on(acc, xs):
        matrix, before = xs
        inner = jnp.einsum('sba,sbc->sac', matrix, acc + before, precision=HIGH)
        out = jnp.einsum('sac,scd->sad', inner, matrix, precision=HIGH)
        return (out, out)
    first = jnp.zeros_like(energy[0])
    unused, rest = lax.scan(carry_on, first, (step_map[1:], previous[1:]))
    new_env = jnp.concatenate([first[None], rest], axis=0)
    return (wave_out, new_env)
```

```python
import functools

import jax
import jax.numpy as jnp
from jax import lax
from jax.experimental import pallas as pl
from jax.experimental.pallas import tpu as pltpu
from jax.sharding import PartitionSpec as P

ITERS = 3
SIDE = 4
CHARGES = 4
BK = 128
HALF = 64
NS = 16
SLOTS = 4
NSEG = 16
ROUNDS = 4
ENTRIES = float(NS * BK * BK)
mean_eps = 1e-06
step_size = 0.5

F32 = jnp.float32
BF16 = jnp.bfloat16
MESH = pl.DeviceIdType.MESH


def split(x):
    high = x.astype(BF16)
    low = (x - high.astype(F32)).astype(BF16)
    return high, low


def beside(x):
    return jnp.concatenate(split(x), axis=1)


def doubled(x):
    row = beside(x)
    return jnp.concatenate([row, row], axis=0)


def product(left, right):
    both = jnp.dot(left, right, preferred_element_type=F32)
    return both[:, :BK] + both[:, BK:]


def fold(x):
    return jnp.sum(x.reshape(x.shape[0] // 8, 8, x.shape[1]), axis=0)


def far_first(i):
    return (2 + i + i // 2 + 2 * (i // 3)) % 4


def near_first(i):
    return i + i // 2 - 2 * (i // 3)


def kernel(
    sector_ref, term_ref, live_ref, wave_hbm, left_hbm, right_hbm, transfer_hbm,
    wave_out, env_out,
    code, place, source, target, mask,
    stage_l, stage_r, stage_w, stage_t, lcat, rcat, inner, waves, image_parts,
    r1, p2, r2, small, small_in, qs, q_in, qdup, qt, s_out, s_in, env_acc,
    load_sem, s1_send, s1_recv, s2_send, s2_recv, g1_send, g2_send, g_recv,
    small_send, small_recv, q_send, q_recv, c_send, c_recv,
):
    seg = lax.axis_index("seg")
    own = lax.axis_index("term")
    x, y = own // SIDE, own % SIDE

    def at(dx, dy):
        return (seg, ((x + dx) % SIDE) * SIDE + (y + dy) % SIDE)

    load_w = pltpu.make_async_copy(wave_hbm.at[0], stage_w, load_sem.at[0])
    load_t = pltpu.make_async_copy(transfer_hbm.at[0, own], stage_t, load_sem.at[1])
    load_w.start()
    load_t.start()
    load_l = [pltpu.make_async_copy(left_hbm.at[0, w], stage_l.at[w], load_sem.at[2 + w]) for w in range(SLOTS)]
    load_r = [pltpu.make_async_copy(right_hbm.at[0, w], stage_r.at[w], load_sem.at[6 + w]) for w in range(SLOTS)]
    for load in load_l + load_r:
        load.start()
    barrier = pltpu.get_barrier_semaphore()
    greeted = 0
    for d in range(1, SIDE):
        pl.semaphore_signal(barrier, inc=1, device_id=at(d, 0), device_id_type=MESH)
        pl.semaphore_signal(barrier, inc=1, device_id=at(0, d), device_id_type=MESH)
        greeted += 2
    for d in (1, 2, 4, 8, 12, 14, 15):
        pl.semaphore_signal(barrier, inc=1, device_id=((seg + d) % NSEG, own), device_id_type=MESH)
        greeted += 1

    for s in range(NS):
        code[s] = sector_ref[s, 0] * CHARGES + sector_ref[s, 1]

    def find(c, carry):
        found = jnp.int32(0)
        for s in range(NS):
            found = jnp.where(code[s] == c, jnp.int32(s), found)
        place[c] = found
        return carry

    lax.fori_loop(0, NS, find, 0)

    def look_up(w, carry):
        up_change, down_change = term_ref[w, 0], term_ref[w, 1]
        alive = live_ref[w].astype(F32)

        def one(s, carry):
            def sector_at(up, down):
                inside = (up >= 0) & (up < CHARGES) & (down >= 0) & (down < CHARGES)
                return inside, place[jnp.where(inside, up * CHARGES + down, 0)]

            up, down = sector_ref[s, 0], sector_ref[s, 1]
            inside, found = sector_at(up - up_change, down - down_change)
            source[w * NS + s] = found
            mask[w * NS + s] = jnp.where(inside, alive, jnp.float32(0))
            target[w * NS + s] = sector_at(up + up_change, down + down_change)[1]
            return carry

        return lax.fori_loop(0, NS, one, carry)

    lax.fori_loop(0, SLOTS, look_up, 0)

    load_w.wait()

    def add_square(t, total):
        v = stage_w[t]
        return total + fold(v * v)

    def scale_from(squares):
        return lax.rsqrt(jnp.sum(squares) / ENTRIES + mean_eps)

    squares = lax.fori_loop(0, NS, add_square, jnp.zeros((8, BK), F32))
    scale = scale_from(squares)

    def set_wave(t, carry):
        waves[0, t] = stage_w[t] * scale
        return carry

    lax.fori_loop(0, NS, set_wave, 0)

    for w in range(SLOTS):
        load_l[w].wait()

        def set_left(s, carry):
            lcat[w, s] = beside(stage_l[w, s])
            return carry

        lax.fori_loop(0, NS, set_left, 0)

    load_t.wait()
    rows = lax.broadcasted_iota(jnp.int32, (BK, BK), 0)
    columns = lax.broadcasted_iota(jnp.int32, (BK, BK), 1)
    qs[0] = stage_t[...] + jnp.where(rows == columns, jnp.float32(1), jnp.float32(0))
    pl.semaphore_wait(barrier, greeted)

    def chain_copy(src, dst, send, recv, k):
        return pltpu.make_async_remote_copy(
            src_ref=src.at[k], dst_ref=dst.at[k], send_sem=send.at[k], recv_sem=recv.at[k],
            device_id=((seg + 2**k) % NSEG, own), device_id_type=MESH,
        )

    def send_map(k):
        @pl.when(seg + 2**k < NSEG)
        def _():
            chain_copy(qs, q_in, q_send, q_recv, k).start()

    def join_map(k):
        q = qs[k]
        qdup[k] = doubled(q)
        qt[k] = beside(q.T)
        if k + 1 < ROUNDS:
            @pl.when(seg >= 2**k)
            def _():
                chain_copy(qs, q_in, q_send, q_recv, k).wait_recv()
                qs[k + 1] = product(beside(q_in[k]), qdup[k])

            @pl.when(seg < 2**k)
            def _():
                qs[k + 1] = q

            @pl.when(seg + 2**k < NSEG)
            def _():
                chain_copy(qs, q_in, q_send, q_recv, k).wait_send()

    send_map(0)

    def s1_copy(it, side, d, chunk, src):
        return pltpu.make_async_remote_copy(
            src_ref=src, dst_ref=r1.at[it, side, d - 1, chunk],
            send_sem=s1_send.at[side, d - 1, chunk], recv_sem=s1_recv.at[side, d - 1, chunk],
            device_id=at(0, d) if side == 0 else at(d, 0), device_id_type=MESH,
        )

    def s2_copy(it, side, d):
        return pltpu.make_async_remote_copy(
            src_ref=p2.at[it, side, d], dst_ref=r2.at[it, side, d - 1],
            send_sem=s2_send.at[side, d - 1], recv_sem=s2_recv.at[side, d - 1],
            device_id=at(d, 0) if side == 0 else at(0, d), device_id_type=MESH,
        )

    def half(side):
        return pl.ds(side * HALF, HALF)

    def small_copy(it, side, d):
        return pltpu.make_async_remote_copy(
            src_ref=small.at[it, side], dst_ref=small_in.at[it, side, d - 1],
            send_sem=small_send.at[it, side, d - 1], recv_sem=small_recv.at[it, side, d - 1],
            device_id=at(0, d) if side == 0 else at(d, 0), device_id_type=MESH,
        )

    def small_start(it, side, value):
        small[it, side] = value
        for d in (2, 1, 3):
            small_copy(it, side, d).start()

    def small_sum(it, side):
        total = small[it, side]
        for d in (1, 2, 3):
            small_copy(it, side, d).wait_recv()
            total = total + small_in[it, side, d - 1]
        return total

    def small_end(it):
        for side in (0, 1):
            for d in (1, 2, 3):
                small_copy(it, side, d).wait_send()

    def gather_copy(it, sector, side, send, device):
        block = waves.at[it, sector, half(side)]
        return pltpu.make_async_remote_copy(
            src_ref=block, dst_ref=block, send_sem=send, recv_sem=g_recv.at[sector, side],
            device_id=device, device_id_type=MESH,
        )

    def arrived(it, sector, side):
        gather_copy(it, sector, side, g1_send.at[0, 0], at(1, 0)).wait_recv()

    def sector_of(dx, dy):
        return ((x + dx) % SIDE) * SIDE + (y + dy) % SIDE

    def forward(it, side, i):
        sector = sector_of(i, 0) if side == 0 else sector_of(0, i)
        return [
            gather_copy(it, sector, side, g2_send.at[side, i, d - 1], at(0, d) if side == 0 else at(d, 0))
            for d in (2, 1, 3)
        ]

    def first_hop(it):
        return [
            gather_copy(it, own, side, g1_send.at[side, d - 1], at(d, 0) if side == 0 else at(0, d))
            for d in (2, 1, 3) for side in (0, 1)
        ]

    def left_half(it, t, squares):
        v = waves[it, t]
        left = jnp.concatenate([lcat[w, target[w * NS + t]] for w in range(SLOTS)], axis=0)
        high, low = split(product(left, doubled(v)))
        for w in range(SLOTS):
            part = slice(w * BK, (w + 1) * BK)
            inner[w, t] = jnp.concatenate([high[part], low[part]], axis=0)
        return squares + fold(v * v)

    def right_half(it, s, scale):
        left = jnp.concatenate([inner[w, source[w * NS + s]] for w in range(SLOTS)], axis=1)
        both = lax.dot_general(left, rcat[s], (((1,), (1,)), ((), ())), preferred_element_type=F32)
        return (both[:BK, :BK] + both[:BK, BK:] + both[BK:, :BK] + both[BK:, BK:]) * scale

    scale = jnp.float32(1)
    for it in range(ITERS):
        if it == 0:
            lax.fori_loop(0, NS, functools.partial(left_half, 0), jnp.zeros((8, BK), F32))
            for w in range(SLOTS):
                load_r[w].wait()

                def set_right(s, carry):
                    high, low = split(stage_r[w, s] * mask[w * NS + s])
                    rcat[s, 0:BK, w * BK:(w + 1) * BK] = high
                    rcat[s, BK:2 * BK, w * BK:(w + 1) * BK] = low
                    return carry

                lax.fori_loop(0, NS, set_right, 0)
        else:
            for side in (0, 1):
                for copy in forward(it, side, 0):
                    copy.start()
            for i in (1, 3, 2):
                for side in (0, 1):
                    arrived(it, sector_of(i, 0) if side == 0 else sector_of(0, i), side)
                    for copy in forward(it, side, i):
                        copy.start()

            def take(q, squares):
                dx, dy = near_first(q // SIDE), near_first(q % SIDE)
                t = sector_of(dx, dy)

                @pl.when(dy != 0)
                def _():
                    arrived(it, t, 0)

                @pl.when(dx != 0)
                def _():
                    arrived(it, t, 1)

                return left_half(it, t, squares)

            squares = lax.fori_loop(0, NS, take, jnp.zeros((8, BK), F32))
            scale = scale_from(squares)
            for copy in first_hop(it):
                copy.wait_send()
            for side in (0, 1):
                for i in range(SIDE):
                    for copy in forward(it, side, i):
                        copy.wait_send()

        def give(q, total):
            dx, dy = far_first(q // SIDE), far_first(q % SIDE)
            sx, sy = (x + dx) % SIDE, (y + dy) % SIDE
            s = sx * SIDE + sy
            block = right_half(it, s, scale)
            image_parts[it, s] = block

            @pl.when(dy != 0)
            def _():
                s1_copy(it, 0, dy, sx, image_parts.at[it, s, half(0)]).start()

            @pl.when(dx != 0)
            def _():
                s1_copy(it, 1, dx, sy, image_parts.at[it, s, half(1)]).start()

            return total + fold(block * waves[it, s])

        total = lax.fori_loop(0, NS, give, jnp.zeros((8, BK), F32))
        small_start(it, 0, total * scale)
        join_map(it)
        if it + 1 < ROUNDS - 1:
            send_map(it + 1)

        def pass_on(i, carry):
            d = far_first(i)
            for side in (0, 1):
                s = sector_of(d, 0) if side == 0 else sector_of(0, d)
                chunk = (x + d) % SIDE if side == 0 else (y + d) % SIDE
                block = image_parts[it, s, half(side)]
                for e in (1, 2, 3):
                    s1_copy(it, side, e, chunk, image_parts.at[it, s, half(side)]).wait_recv()
                    block = block + r1[it, side, e - 1, chunk]
                p2[it, side, d] = block

                @pl.when(d != 0)
                def _():
                    s2_copy(it, side, d).start()

            return carry

        lax.fori_loop(0, SIDE, pass_on, 0)
        small_start(it, 1, small_sum(it, 0))
        halves = []
        for side in (0, 1):
            block = p2[it, side, 0]
            for d in (1, 2, 3):
                s2_copy(it, side, d).wait_recv()
                block = block + r2[it, side, d - 1]
            halves.append(block)
        image = jnp.concatenate(halves, axis=0)
        theta = jnp.sum(small_sum(it, 1)) / ENTRIES
        wave = waves[it, own] * scale
        wave = wave - step_size * (image - theta * wave)
        waves[it + 1, own] = wave
        if it + 1 < ITERS:
            for copy in first_hop(it + 1):
                copy.start()
        else:
            small_start(ITERS, 0, fold(wave * wave))

        for side in (0, 1):
            for d in (1, 2, 3):
                s2_copy(it, side, d).wait_send()
                for chunk in range(SIDE):
                    s1_copy(it, side, d, chunk, p2.at[it, side, d]).wait_send()
        small_end(it)

    join_map(ROUNDS - 1)
    energy = product(beside(wave.T), doubled(image))
    small_start(ITERS, 1, small_sum(ITERS, 0))
    scale = scale_from(small_sum(ITERS, 1))
    small_end(ITERS)
    wave_out[0, 0] = wave * scale
    energy = energy * (scale / BK)

    env_acc[...] = jnp.zeros((BK, BK), F32)
    for k in range(ROUNDS):
        @pl.when(seg + 2**k < NSEG)
        def _():
            s_out[k] = env_acc[...] + energy
            chain_copy(s_out, s_in, c_send, c_recv, k).start()

        @pl.when(seg >= 2**k)
        def _():
            chain_copy(s_out, s_in, c_send, c_recv, k).wait_recv()
            half_way = product(beside(s_in[k]), qdup[k])
            env_acc[...] += product(qt[k], doubled(half_way))

    env_out[0, 0] = env_acc[...]
    for k in range(ROUNDS):
        @pl.when(seg + 2**k < NSEG)
        def _():
            chain_copy(s_out, s_in, c_send, c_recv, k).wait_send()


def shards(wave_in, env_left, env_right, sector_charge, term_charge, term_live, transfer):
    smem = pl.BlockSpec(memory_space=pltpu.SMEM)
    vmem = pl.BlockSpec(memory_space=pltpu.VMEM)
    hbm = pl.BlockSpec(memory_space=pl.ANY)
    dma = pltpu.SemaphoreType.DMA
    block = jax.ShapeDtypeStruct((1, 1, BK, BK), F32)
    return pl.pallas_call(
        kernel,
        out_shape=(block, block),
        in_specs=[smem, smem, smem, hbm, hbm, hbm, hbm],
        out_specs=(vmem, vmem),
        scratch_shapes=[
            pltpu.SMEM((NS,), jnp.int32),
            pltpu.SMEM((NS,), jnp.int32),
            pltpu.SMEM((SLOTS * NS,), jnp.int32),
            pltpu.SMEM((SLOTS * NS,), jnp.int32),
            pltpu.SMEM((SLOTS * NS,), F32),
            pltpu.VMEM((SLOTS, NS, BK, BK), F32),
            pltpu.VMEM((SLOTS, NS, BK, BK), F32),
            pltpu.VMEM((NS, BK, BK), F32),
            pltpu.VMEM((BK, BK), F32),
            pltpu.VMEM((SLOTS, NS, BK, 2 * BK), BF16),
            pltpu.VMEM((NS, 2 * BK, SLOTS * BK), BF16),
            pltpu.VMEM((SLOTS, NS, 2 * BK, BK), BF16),
            pltpu.VMEM((ITERS + 1, NS, BK, BK), F32),
            pltpu.VMEM((ITERS, NS, BK, BK), F32),
            pltpu.VMEM((ITERS, 2, SIDE - 1, SIDE, HALF, BK), F32),
            pltpu.VMEM((ITERS, 2, SIDE, HALF, BK), F32),
            pltpu.VMEM((ITERS, 2, SIDE - 1, HALF, BK), F32),
            pltpu.VMEM((ITERS + 1, 2, 8, BK), F32),
            pltpu.VMEM((ITERS + 1, 2, SIDE - 1, 8, BK), F32),
            pltpu.VMEM((ROUNDS, BK, BK), F32),
            pltpu.VMEM((ROUNDS - 1, BK, BK), F32),
            pltpu.VMEM((ROUNDS, 2 * BK, 2 * BK), BF16),
            pltpu.VMEM((ROUNDS, BK, 2 * BK), BF16),
            pltpu.VMEM((ROUNDS, BK, BK), F32),
            pltpu.VMEM((ROUNDS, BK, BK), F32),
            pltpu.VMEM((BK, BK), F32),
            dma((2 + 2 * SLOTS,)),
            dma((2, SIDE - 1, SIDE)),
            dma((2, SIDE - 1, SIDE)),
            dma((2, SIDE - 1)),
            dma((2, SIDE - 1)),
            dma((2, SIDE - 1)),
            dma((2, SIDE, SIDE - 1)),
            dma((NS, 2)),
            dma((ITERS + 1, 2, SIDE - 1)),
            dma((ITERS + 1, 2, SIDE - 1)),
            dma((ROUNDS - 1,)),
            dma((ROUNDS - 1,)),
            dma((ROUNDS,)),
            dma((ROUNDS,)),
        ],
        compiler_params=pltpu.CompilerParams(
            collective_id=0, has_side_effects=True, vmem_limit_bytes=56 * 1024 * 1024
        ),
    )(sector_charge, term_charge, term_live, wave_in, env_left, env_right, transfer)


def solution(mesh):
    in_specs = (
        P("seg", None, None, None),
        P("seg", "term", None, None, None),
        P("seg", "term", None, None, None),
        P(),
        P("term", None),
        P("term"),
        P("seg", None, None, None),
    )
    out_specs = (P("seg", "term", None, None), P("seg", "term", None, None))
    return jax.shard_map(shards, mesh=mesh, in_specs=in_specs, out_specs=out_specs, check_vma=False)
```

```python
import functools

import jax
import jax.numpy as jnp
from jax import lax
from jax.experimental import pallas as pl
from jax.experimental.pallas import tpu as pltpu
from jax.sharding import PartitionSpec as P

ITERS = 3
SIDE = 4
CHARGES = 4
BK = 128
HALF = 64
NS = 16
SLOTS = 4
NSEG = 16
CHIPS = NSEG // 2
ENTRIES = float(NS * BK * BK)
mean_eps = 1e-06
step_size = 0.5

F32 = jnp.float32
BF16 = jnp.bfloat16
MESH = pl.DeviceIdType.MESH


def split(x):
    high = x.astype(BF16)
    low = (x - high.astype(F32)).astype(BF16)
    return high, low


def beside(x):
    return jnp.concatenate(split(x), axis=1)


def doubled(x):
    row = beside(x)
    return jnp.concatenate([row, row], axis=0)


def product(left, right):
    both = jnp.dot(left, right, preferred_element_type=F32)
    return both[:, :BK] + both[:, BK:]


def fold(x):
    return jnp.sum(x.reshape(x.shape[0] // 8, 8, x.shape[1]), axis=0)


def far_first(i):
    return (2 + i + i // 2 + 2 * (i // 3)) % 4


def near_first(i):
    return i + i // 2 - 2 * (i // 3)


def by_shells(q):
    past = [(q + 9) // 16, (q + 4) // 16, (q + 1) // 16]
    r = past[0] + past[1] + past[2]
    m = q - 7 * past[0] - 5 * past[1] - 3 * past[2]
    below = (m + 4 + r) // 8
    return r + below * (m - 3 + r), r + (1 - below) * m


def kernel(
    sector_ref, term_ref, live_ref, wave_hbm, left_hbm, right_hbm, transfer_hbm,
    out,
    code, place, source, target, mask,
    stage_l, stage_r, stage_t, lcat, rcat, inner, waves, image_parts, images,
    r1, p2, r2, small, small_in, norm_out, norm_in,
    t_out, t_in, pair_out, pair_in, tdup, tt, wdup, wt, e_out, e_in, c_out, c_in, f_out, f_in, n_out, n_in,
    load_sem, s1_send, s1_recv, s2_send, s2_recv, g1_send, g2_send, g_recv,
    small_send, small_recv, norm_send, norm_recv, core_send, core_recv, pair_send, pair_recv, f_send, f_recv,
):
    seg = lax.axis_index("seg")
    own = lax.axis_index("term")
    x, y = own // SIDE, own % SIDE
    z, core = seg // 2, seg % 2

    def at(dx, dy):
        return (seg, ((x + dx) % SIDE) * SIDE + (y + dy) % SIDE)

    other_core = (seg + 1 - 2 * core, own)

    load_w = pltpu.make_async_copy(wave_hbm.at[0], waves.at[0], load_sem.at[0])
    load_t = pltpu.make_async_copy(transfer_hbm.at[0, own], stage_t, load_sem.at[1])
    load_w.start()
    load_t.start()
    load_l = [pltpu.make_async_copy(left_hbm.at[0, w], stage_l.at[w], load_sem.at[2 + w]) for w in range(SLOTS)]
    load_r = [pltpu.make_async_copy(right_hbm.at[0, w], stage_r.at[w], load_sem.at[6 + w]) for w in range(SLOTS)]
    for load in load_l + load_r:
        load.start()
    barrier = pltpu.get_barrier_semaphore()
    others = [(dx, dy) for dx in (2, 1, 3, 0) for dy in (2, 1, 3, 0) if (dx, dy) != (0, 0)]
    for dx, dy in others:
        pl.semaphore_signal(barrier, inc=1, device_id=at(dx, dy), device_id_type=MESH)
    for d in range(1, CHIPS):
        pl.semaphore_signal(barrier, inc=1, device_id=((seg + 2 * d) % NSEG, own), device_id_type=MESH)
    pl.semaphore_signal(barrier, inc=1, device_id=other_core, device_id_type=MESH)
    greeted = len(others) + CHIPS

    for s in range(NS):
        code[s] = sector_ref[0, s] * CHARGES + sector_ref[1, s]

    def find(c, carry):
        found = jnp.int32(0)
        for s in range(NS):
            found = jnp.where(code[s] == c, jnp.int32(s), found)
        place[c] = found
        return carry

    lax.fori_loop(0, NS, find, 0)

    def look_up(w, carry):
        up_change, down_change = term_ref[0, w], term_ref[1, w]
        alive = live_ref[w].astype(F32)

        def one(s, carry):
            def sector_at(up, down):
                inside = (up >= 0) & (up < CHARGES) & (down >= 0) & (down < CHARGES)
                return inside, place[jnp.where(inside, up * CHARGES + down, 0)]

            up, down = sector_ref[0, s], sector_ref[1, s]
            inside, found = sector_at(up - up_change, down - down_change)
            source[w * NS + s] = found
            mask[w * NS + s] = jnp.where(inside, alive, jnp.float32(0))
            target[w * NS + s] = sector_at(up + up_change, down + down_change)[1]
            return carry

        return lax.fori_loop(0, NS, one, carry)

    lax.fori_loop(0, SLOTS, look_up, 0)

    load_w.wait()

    def add_square(t, total):
        v = waves[0, t]
        return total + fold(v * v)

    def scale_from(squares):
        return lax.rsqrt(jnp.sum(squares) / ENTRIES + mean_eps)

    zero = jnp.zeros((8, BK), F32)
    squares = lax.fori_loop(0, NS, add_square, zero, unroll=2)
    scale = scale_from(squares)

    for w in range(SLOTS):
        load_l[w].wait()

        def set_left(s, carry):
            lcat[w, s] = beside(stage_l[w, s])
            return carry

        lax.fori_loop(0, NS, set_left, 0, unroll=2)

    def core_copy(src, dst, k):
        return pltpu.make_async_remote_copy(
            src_ref=src, dst_ref=dst, send_sem=core_send.at[k], recv_sem=core_recv.at[k],
            device_id=other_core, device_id_type=MESH,
        )

    def up_copy(src, dst, send, recv, d):
        return pltpu.make_async_remote_copy(
            src_ref=src, dst_ref=dst.at[d - 1], send_sem=send.at[d - 1], recv_sem=recv.at[d - 1],
            device_id=((seg + 2 * d) % NSEG, own), device_id_type=MESH,
        )

    load_t.wait()
    rows = lax.broadcasted_iota(jnp.int32, (BK, BK), 0)
    columns = lax.broadcasted_iota(jnp.int32, (BK, BK), 1)
    t_out[...] = stage_t[...] + jnp.where(rows == columns, jnp.float32(1), jnp.float32(0))
    pl.semaphore_wait(barrier, greeted)

    @pl.when(core == 0)
    def _():
        core_copy(t_out, t_in, 0).start()

    def set_map(d, value):
        wdup[d - 1] = doubled(value)
        wt[d - 1] = beside(value.T)

    def chain_step(it):
        @pl.when(core == 1)
        def _():
            if it == 0:
                own_map = t_out[...]
                tdup[...] = doubled(own_map)
                tt[...] = beside(own_map.T)
                core_copy(t_out, t_in, 0).wait_recv()
                lower_map = t_in[...]
                set_map(1, lower_map)
                pair_out[...] = product(beside(lower_map), tdup[...])
                for d in range(1, CHIPS - 1):
                    @pl.when((z >= 1) & (z + d < CHIPS))
                    def _():
                        up_copy(pair_out, pair_in, pair_send, pair_recv, d).start()
            else:
                for d in ((2, 3, 4) if it == 1 else (5, 6, 7)):
                    @pl.when(z >= d)
                    def _():
                        up_copy(pair_out, pair_in, pair_send, pair_recv, d - 1).wait_recv()
                        set_map(d, product(beside(pair_in[d - 2]), wdup[d - 2]))

    def s1_copy(it, side, d, chunk, src):
        return pltpu.make_async_remote_copy(
            src_ref=src, dst_ref=r1.at[it, side, d - 1, chunk],
            send_sem=s1_send.at[side, d - 1, chunk], recv_sem=s1_recv.at[side, d - 1, chunk],
            device_id=at(0, d) if side == 0 else at(d, 0), device_id_type=MESH,
        )

    def s2_copy(it, side, d):
        return pltpu.make_async_remote_copy(
            src_ref=p2.at[it, side, d], dst_ref=r2.at[it, side, d - 1],
            send_sem=s2_send.at[side, d - 1], recv_sem=s2_recv.at[side, d - 1],
            device_id=at(d, 0) if side == 0 else at(0, d), device_id_type=MESH,
        )

    def half(side):
        return pl.ds(side * HALF, HALF)

    def small_copy(it, side, d):
        return pltpu.make_async_remote_copy(
            src_ref=small.at[it, side], dst_ref=small_in.at[it, side, d - 1],
            send_sem=small_send.at[it, side, d - 1], recv_sem=small_recv.at[it, side, d - 1],
            device_id=at(0, d) if side == 0 else at(d, 0), device_id_type=MESH,
        )

    def small_start(it, side, value):
        small[it, side] = value
        for d in (2, 1, 3):
            small_copy(it, side, d).start()

    def small_sum(it, side):
        total = small[it, side]
        for d in (1, 2, 3):
            small_copy(it, side, d).wait_recv()
            total = total + small_in[it, side, d - 1]
        return total

    def small_end(it):
        for side in (0, 1):
            for d in (1, 2, 3):
                small_copy(it, side, d).wait_send()

    def norm_copy(dx, dy):
        slot = dx * SIDE + dy
        return pltpu.make_async_remote_copy(
            src_ref=norm_out, dst_ref=norm_in.at[slot], send_sem=norm_send.at[slot], recv_sem=norm_recv.at[slot],
            device_id=at(dx, dy), device_id_type=MESH,
        )

    def gather_copy(it, sector, side, send, device):
        block = images.at[it, sector, half(side)]
        return pltpu.make_async_remote_copy(
            src_ref=block, dst_ref=block, send_sem=send, recv_sem=g_recv.at[sector, side],
            device_id=device, device_id_type=MESH,
        )

    def arrived(it, sector, side):
        gather_copy(it, sector, side, g1_send.at[0, 0], at(1, 0)).wait_recv()

    def sector_of(dx, dy):
        return ((x + dx) % SIDE) * SIDE + (y + dy) % SIDE

    def forward(it, side, i):
        sector = sector_of(i, 0) if side == 0 else sector_of(0, i)
        return [
            gather_copy(it, sector, side, g2_send.at[side, i, d - 1], at(0, d) if side == 0 else at(d, 0))
            for d in (2, 1, 3)
        ]

    def first_hop(it):
        return [
            gather_copy(it, own, side, g1_send.at[side, d - 1], at(d, 0) if side == 0 else at(0, d))
            for d in (2, 1, 3) for side in (0, 1)
        ]

    def left_half(t, v):
        left = jnp.concatenate([lcat[w, target[w * NS + t]] for w in range(SLOTS)], axis=0)
        high, low = split(product(left, doubled(v)))
        for w in range(SLOTS):
            part = slice(w * BK, (w + 1) * BK)
            inner[w, t] = jnp.concatenate([high[part], low[part]], axis=0)

    def right_half(s, scale):
        left = jnp.concatenate([inner[w, source[w * NS + s]] for w in range(SLOTS)], axis=1)
        both = lax.dot_general(left, rcat[s], (((1,), (1,)), ((), ())), preferred_element_type=F32)
        return (both[:BK, :BK] + both[:BK, BK:] + both[BK:, :BK] + both[BK:, BK:]) * scale

    for it in range(ITERS):
        if it == 0:
            def begin(t, carry):
                v = waves[0, t] * scale
                waves[0, t] = v
                left_half(t, v)
                return carry

            lax.fori_loop(0, NS, begin, 0, unroll=2)
            scale = jnp.float32(1)
            for w in range(SLOTS):
                load_r[w].wait()

                def set_right(s, carry):
                    high, low = split(stage_r[w, s] * mask[w * NS + s])
                    rcat[s, 0:BK, w * BK:(w + 1) * BK] = high
                    rcat[s, BK:2 * BK, w * BK:(w + 1) * BK] = low
                    return carry

                lax.fori_loop(0, NS, set_right, 0, unroll=2)
        else:
            for side in (0, 1):
                for copy in forward(it - 1, side, 0):
                    copy.start()
            for i in (1, 3, 2):
                for side in (0, 1):
                    arrived(it - 1, sector_of(i, 0) if side == 0 else sector_of(0, i), side)
                    for copy in forward(it - 1, side, i):
                        copy.start()
            theta = jnp.sum(small_sum(it - 1, 1)) / ENTRIES

            def take(p, squares):
                blocks = []
                for q in (2 * p, 2 * p + 1):
                    dx, dy = near_first(q // SIDE), near_first(q % SIDE)
                    t = sector_of(dx, dy)
                    blocks.append(t)

                    @pl.when(dy != 0)
                    def _():
                        arrived(it - 1, t, 0)

                    @pl.when(dx != 0)
                    def _():
                        arrived(it - 1, t, 1)

                values = []
                for t in blocks:
                    wave = waves[it - 1, t] * scale
                    values.append(wave - step_size * (images[it - 1, t] - theta * wave))
                for t, v in zip(blocks, values):
                    left_half(t, v)
                for t, v in zip(blocks, values):
                    waves[it, t] = v
                    squares = squares + fold(v * v)
                return squares

            squares = lax.fori_loop(0, NS // 2, take, zero)
            scale = scale_from(squares)
            for copy in first_hop(it - 1):
                copy.wait_send()
            for side in (0, 1):
                for i in range(SIDE):
                    for copy in forward(it - 1, side, i):
                        copy.wait_send()
            small_end(it - 1)

        def give(p, total):
            places = []
            for q in (2 * p, 2 * p + 1):
                i, k = by_shells(q)
                places.append((far_first(i), far_first(k)))
            made = []
            for dx, dy in places:
                made.append(right_half(sector_of(dx, dy), scale))
            for (dx, dy), block in zip(places, made):
                image_parts[it, sector_of(dx, dy)] = block
            for (dx, dy), block in zip(places, made):
                sx, sy = (x + dx) % SIDE, (y + dy) % SIDE
                s = sx * SIDE + sy

                @pl.when(dy != 0)
                def _():
                    s1_copy(it, 0, dy, sx, image_parts.at[it, s, half(0)]).start()

                @pl.when(dx != 0)
                def _():
                    s1_copy(it, 1, dx, sy, image_parts.at[it, s, half(1)]).start()

                total = total + fold(block * waves[it, s])
            return total

        total = lax.fori_loop(0, NS // 2, give, zero)
        small_start(it, 0, total * scale)
        chain_step(it)

        def pass_on(i, carry):
            d = far_first(i)
            for side in (0, 1):
                s = sector_of(d, 0) if side == 0 else sector_of(0, d)
                chunk = (x + d) % SIDE if side == 0 else (y + d) % SIDE
                block = image_parts[it, s, half(side)]
                for e in (1, 2, 3):
                    s1_copy(it, side, e, chunk, image_parts.at[it, s, half(side)]).wait_recv()
                    block = block + r1[it, side, e - 1, chunk]
                p2[it, side, d] = block

                @pl.when(d != 0)
                def _():
                    s2_copy(it, side, d).start()

            return carry

        lax.fori_loop(0, SIDE, pass_on, 0)
        small_start(it, 1, small_sum(it, 0))
        halves = []
        for side in (0, 1):
            block = p2[it, side, 0]
            for d in (1, 2, 3):
                s2_copy(it, side, d).wait_recv()
                block = block + r2[it, side, d - 1]
            halves.append(block)
        image = jnp.concatenate(halves, axis=0)
        if it + 1 < ITERS:
            images[it, own] = image
            for copy in first_hop(it):
                copy.start()
        else:
            theta = jnp.sum(small_sum(it, 1)) / ENTRIES
            wave = waves[it, own] * scale
            wave = wave - step_size * (image - theta * wave)
            norm_out[...] = fold(wave * wave)
            for dx, dy in others:
                norm_copy(dx, dy).start()

        for side in (0, 1):
            for d in (1, 2, 3):
                s2_copy(it, side, d).wait_send()
                for chunk in range(SIDE):
                    s1_copy(it, side, d, chunk, p2.at[it, side, d]).wait_send()

    energy = product(beside(wave.T), doubled(image))

    @pl.when(core == 0)
    def _():
        e_out[...] = energy
        core_copy(e_out, e_in, 1).start()

    @pl.when(core == 1)
    def _():
        core_copy(e_out, e_in, 1).wait_recv()
        n_out[...] = product(tt[...], doubled(product(beside(e_in[...]), tdup[...])))

    squares = norm_out[...]
    for dx, dy in others:
        norm_copy(dx, dy).wait_recv()
        squares = squares + norm_in[dx * SIDE + dy]
    scale = scale_from(squares)
    energy_scale = scale / BK

    @pl.when(core == 0)
    def _():
        c_out[...] = jnp.full((8, BK), energy_scale, F32)
        core_copy(c_out, c_in, 2).start()

    out[0] = wave * scale

    @pl.when(core == 1)
    def _():
        core_copy(c_out, c_in, 2).wait_recv()
        lower = n_out[...] * c_in[0:1, 0:1]
        f_out[...] = energy * energy_scale + lower
        for d in range(CHIPS - 1, 0, -1):
            @pl.when(z + d < CHIPS)
            def _():
                up_copy(f_out, f_in, f_send, f_recv, d).start()

        out[1] = lower
        n_out[...] = jnp.zeros((BK, BK), F32)
        for d in range(1, CHIPS):
            @pl.when(z >= d)
            def _():
                up_copy(f_out, f_in, f_send, f_recv, d).wait_recv()
                n_out[...] += product(wt[d - 1], doubled(product(beside(f_in[d - 1]), wdup[d - 1])))

        core_copy(n_out, n_in, 3).start()
        out[1] += product(tt[...], doubled(product(beside(n_out[...]), tdup[...])))
        for d in range(1, CHIPS):
            @pl.when(z + d < CHIPS)
            def _():
                up_copy(f_out, f_in, f_send, f_recv, d).wait_send()

            if d < CHIPS - 1:
                @pl.when((z >= 1) & (z + d < CHIPS))
                def _():
                    up_copy(pair_out, pair_in, pair_send, pair_recv, d).wait_send()

        core_copy(n_out, n_in, 3).wait_send()

    @pl.when(core == 0)
    def _():
        core_copy(t_out, t_in, 0).wait_send()
        core_copy(e_out, e_in, 1).wait_send()
        core_copy(c_out, c_in, 2).wait_send()
        core_copy(n_out, n_in, 3).wait_recv()
        out[1] = n_in[...]

    for dx, dy in others:
        norm_copy(dx, dy).wait_send()
    small_end(ITERS - 1)


def shards(wave_in, env_left, env_right, sector_charge, term_charge, term_live, transfer):
    smem = pl.BlockSpec(memory_space=pltpu.SMEM)
    vmem = pl.BlockSpec(memory_space=pltpu.VMEM)
    hbm = pl.BlockSpec(memory_space=pl.ANY)
    dma = pltpu.SemaphoreType.DMA
    square = pltpu.VMEM((BK, BK), F32)
    tile = pltpu.VMEM((8, BK), F32)
    both = pl.pallas_call(
        kernel,
        out_shape=jax.ShapeDtypeStruct((2, BK, BK), F32),
        in_specs=[smem, smem, smem, hbm, hbm, hbm, hbm],
        out_specs=vmem,
        scratch_shapes=[
            pltpu.SMEM((NS,), jnp.int32),
            pltpu.SMEM((NS,), jnp.int32),
            pltpu.SMEM((SLOTS * NS,), jnp.int32),
            pltpu.SMEM((SLOTS * NS,), jnp.int32),
            pltpu.SMEM((SLOTS * NS,), F32),
            pltpu.VMEM((SLOTS, NS, BK, BK), F32),
            pltpu.VMEM((SLOTS, NS, BK, BK), F32),
            square,
            pltpu.VMEM((SLOTS, NS, BK, 2 * BK), BF16),
            pltpu.VMEM((NS, 2 * BK, SLOTS * BK), BF16),
            pltpu.VMEM((SLOTS, NS, 2 * BK, BK), BF16),
            pltpu.VMEM((ITERS, NS, BK, BK), F32),
            pltpu.VMEM((ITERS, NS, BK, BK), F32),
            pltpu.VMEM((ITERS - 1, NS, BK, BK), F32),
            pltpu.VMEM((ITERS, 2, SIDE - 1, SIDE, HALF, BK), F32),
            pltpu.VMEM((ITERS, 2, SIDE, HALF, BK), F32),
            pltpu.VMEM((ITERS, 2, SIDE - 1, HALF, BK), F32),
            pltpu.VMEM((ITERS, 2, 8, BK), F32),
            pltpu.VMEM((ITERS, 2, SIDE - 1, 8, BK), F32),
            tile,
            pltpu.VMEM((NS, 8, BK), F32),
            square,
            square,
            square,
            pltpu.VMEM((CHIPS - 2, BK, BK), F32),
            pltpu.VMEM((2 * BK, 2 * BK), BF16),
            pltpu.VMEM((BK, 2 * BK), BF16),
            pltpu.VMEM((CHIPS - 1, 2 * BK, 2 * BK), BF16),
            pltpu.VMEM((CHIPS - 1, BK, 2 * BK), BF16),
            square,
            square,
            tile,
            tile,
            square,
            pltpu.VMEM((CHIPS - 1, BK, BK), F32),
            square,
            square,
            dma((2 + 2 * SLOTS,)),
            dma((2, SIDE - 1, SIDE)),
            dma((2, SIDE - 1, SIDE)),
            dma((2, SIDE - 1)),
            dma((2, SIDE - 1)),
            dma((2, SIDE - 1)),
            dma((2, SIDE, SIDE - 1)),
            dma((NS, 2)),
            dma((ITERS, 2, SIDE - 1)),
            dma((ITERS, 2, SIDE - 1)),
            dma((NS,)),
            dma((NS,)),
            dma((4,)),
            dma((4,)),
            dma((CHIPS - 2,)),
            dma((CHIPS - 2,)),
            dma((CHIPS - 1,)),
            dma((CHIPS - 1,)),
        ],
        compiler_params=pltpu.CompilerParams(
            collective_id=0, has_side_effects=True, vmem_limit_bytes=56 * 1024 * 1024
        ),
    )(sector_charge.T, term_charge.T, term_live, wave_in, env_left, env_right, transfer)
    block = (1, 1, BK, BK)
    return both[0].reshape(block), both[1].reshape(block)


def solution(mesh):
    in_specs = (
        P("seg", None, None, None),
        P("seg", "term", None, None, None),
        P("seg", "term", None, None, None),
        P(),
        P("term", None),
        P("term"),
        P("seg", None, None, None),
    )
    out_specs = (P("seg", "term", None, None), P("seg", "term", None, None))
    return jax.shard_map(shards, mesh=mesh, in_specs=in_specs, out_specs=out_specs, check_vma=False)
```

```python
import functools

import jax
import jax.numpy as jnp
from jax import lax
from jax.experimental import pallas as pl
from jax.experimental.pallas import tpu as pltpu
from jax.sharding import PartitionSpec as P

ITERS = 3
SIDE = 4
CHARGES = 4
BK = 128
HALF = 64
NS = 16
SLOTS = 4
NSEG = 16
CHIPS = NSEG // 2
ENTRIES = float(NS * BK * BK)
mean_eps = 1e-06
step_size = 0.5

F32 = jnp.float32
BF16 = jnp.bfloat16
MESH = pl.DeviceIdType.MESH


def split(x):
    high = x.astype(BF16)
    low = (x - high.astype(F32)).astype(BF16)
    return high, low


def beside(x):
    return jnp.concatenate(split(x), axis=1)


def doubled(x):
    row = beside(x)
    return jnp.concatenate([row, row], axis=0)


def product(left, right):
    both = jnp.dot(left, right, preferred_element_type=F32)
    return both[:, :BK] + both[:, BK:]


def fold(x):
    return jnp.sum(x.reshape(x.shape[0] // 8, 8, x.shape[1]), axis=0)


def first_shell(r):
    return [(r, k) for k in range(r, SIDE)] + [(k, r) for k in range(r + 1, SIDE)]


def last_shell(r):
    return [(r, k) for k in range(r)] + [(k, r) for k in range(r)] + [(r, r)]


def kernel(
    sector_hbm, term_hbm, live_hbm, wave_hbm, left_hbm, right_hbm, transfer_hbm,
    out,
    sector_ref, term_ref, live_ref, code, place, source, target, mask,
    stage_l, stage_r, stage_t, lcat, rcat, inner, waves, image_parts, images,
    r1, p2, r2, small, small_in, norm_out, norm_in,
    t_out, t_in, pair_out, pair_in, tdup, tt, wdup, wt, e_out, e_in, c_out, c_in, f_out, f_in, n_out, n_in,
    load_sem, s1_send, s1_recv, s2_send, s2_recv, g_send, g_recv,
    small_send, small_recv, norm_send, norm_recv, core_send, core_recv, pair_send, pair_recv, f_send, f_recv,
):
    seg = lax.axis_index("seg")
    own = lax.axis_index("term")
    x, y = own // SIDE, own % SIDE
    z, core = seg // 2, seg % 2

    def at(dx, dy):
        return (seg, ((x + dx) % SIDE) * SIDE + (y + dy) % SIDE)

    other_core = (seg + 1 - 2 * core, own)

    load_w = pltpu.make_async_copy(wave_hbm.at[0], waves.at[0], load_sem.at[0])
    load_t = pltpu.make_async_copy(transfer_hbm.at[0, own], stage_t, load_sem.at[1])
    load_i = [
        pltpu.make_async_copy(sector_hbm, sector_ref, load_sem.at[10]),
        pltpu.make_async_copy(term_hbm, term_ref, load_sem.at[11]),
        pltpu.make_async_copy(live_hbm, live_ref, load_sem.at[12]),
    ]
    for load in load_i:
        load.start()
    load_w.start()
    load_t.start()
    load_l = [pltpu.make_async_copy(left_hbm.at[0, w], stage_l.at[w], load_sem.at[2 + w]) for w in range(SLOTS)]
    load_r = [pltpu.make_async_copy(right_hbm.at[0, w], stage_r.at[w], load_sem.at[6 + w]) for w in range(SLOTS)]
    for load in load_l + load_r:
        load.start()
    barrier = pltpu.get_barrier_semaphore()
    others = [(dx, dy) for dx in (2, 1, 3, 0) for dy in (2, 1, 3, 0) if (dx, dy) != (0, 0)]
    for dx, dy in others:
        pl.semaphore_signal(barrier, inc=1, device_id=at(dx, dy), device_id_type=MESH)
    for d in range(1, CHIPS):
        pl.semaphore_signal(barrier, inc=1, device_id=((seg + 2 * d) % NSEG, own), device_id_type=MESH)
    pl.semaphore_signal(barrier, inc=1, device_id=other_core, device_id_type=MESH)
    greeted = len(others) + CHIPS

    for load in load_i:
        load.wait()
    for s in range(NS):
        code[s] = sector_ref[0, s] * CHARGES + sector_ref[1, s]

    def find(c, carry):
        found = jnp.int32(0)
        for s in range(NS):
            found = jnp.where(code[s] == c, jnp.int32(s), found)
        place[c] = found
        return carry

    lax.fori_loop(0, NS, find, 0)

    def look_up(w, carry):
        up_change, down_change = term_ref[0, w], term_ref[1, w]
        alive = live_ref[w].astype(F32)

        def one(s, carry):
            def sector_at(up, down):
                inside = (up >= 0) & (up < CHARGES) & (down >= 0) & (down < CHARGES)
                return inside, place[jnp.where(inside, up * CHARGES + down, 0)]

            up, down = sector_ref[0, s], sector_ref[1, s]
            inside, found = sector_at(up - up_change, down - down_change)
            source[w * NS + s] = found
            mask[w * NS + s] = jnp.where(inside, alive, jnp.float32(0))
            target[w * NS + s] = sector_at(up + up_change, down + down_change)[1]
            return carry

        return lax.fori_loop(0, NS, one, carry)

    lax.fori_loop(0, SLOTS, look_up, 0)

    load_w.wait()

    def add_square(t, total):
        v = waves[0, t]
        return total + fold(v * v)

    def scale_from(squares):
        return lax.rsqrt(jnp.sum(squares) / ENTRIES + mean_eps)

    zero = jnp.zeros((8, BK), F32)
    squares = lax.fori_loop(0, NS, add_square, zero, unroll=2)
    scale = scale_from(squares)

    for w in range(SLOTS):
        load_l[w].wait()

        def set_left(s, carry):
            lcat[w, s] = beside(stage_l[w, s])
            return carry

        lax.fori_loop(0, NS, set_left, 0, unroll=2)

    def core_copy(src, dst, k):
        return pltpu.make_async_remote_copy(
            src_ref=src, dst_ref=dst, send_sem=core_send.at[k], recv_sem=core_recv.at[k],
            device_id=other_core, device_id_type=MESH,
        )

    def up_copy(src, dst, send, recv, d):
        return pltpu.make_async_remote_copy(
            src_ref=src, dst_ref=dst.at[d - 1], send_sem=send.at[d - 1], recv_sem=recv.at[d - 1],
            device_id=((seg + 2 * d) % NSEG, own), device_id_type=MESH,
        )

    load_t.wait()
    rows = lax.broadcasted_iota(jnp.int32, (BK, BK), 0)
    columns = lax.broadcasted_iota(jnp.int32, (BK, BK), 1)
    t_out[...] = stage_t[...] + jnp.where(rows == columns, jnp.float32(1), jnp.float32(0))
    pl.semaphore_wait(barrier, greeted)

    @pl.when(core == 0)
    def _():
        core_copy(t_out, t_in, 0).start()

    def set_map(d, value):
        wdup[d - 1] = doubled(value)
        wt[d - 1] = beside(value.T)

    def first_maps():
        @pl.when(core == 1)
        def _():
            own_map = t_out[...]
            tdup[...] = doubled(own_map)
            tt[...] = beside(own_map.T)
            core_copy(t_out, t_in, 0).wait_recv()
            lower_map = t_in[...]
            set_map(1, lower_map)
            pair_out[...] = product(beside(lower_map), tdup[...])
            for d in range(1, CHIPS - 1):
                @pl.when((z >= 1) & (z + d < CHIPS))
                def _():
                    up_copy(pair_out, pair_in, pair_send, pair_recv, d).start()

    def more_maps(which):
        for d in which:
            @pl.when((core == 1) & (z >= d))
            def _():
                up_copy(pair_out, pair_in, pair_send, pair_recv, d - 1).wait_recv()
                set_map(d, product(beside(pair_in[d - 2]), wdup[d - 2]))

    def half(side):
        return pl.ds(side * HALF, HALF)

    def along(side, d):
        return at(0, d) if side == 0 else at(d, 0)

    def s1_copy(it, side, d, chunk):
        sector = chunk * SIDE + (y + d) % SIDE if side == 0 else ((x + d) % SIDE) * SIDE + chunk
        return pltpu.make_async_remote_copy(
            src_ref=image_parts.at[it, sector, half(side)], dst_ref=r1.at[it, side, d - 1, chunk],
            send_sem=s1_send.at[0], recv_sem=s1_recv.at[chunk],
            device_id=along(side, d), device_id_type=MESH,
        )

    def s2_copy(it, side, d, chunk, slot):
        return pltpu.make_async_remote_copy(
            src_ref=p2.at[it, side, chunk], dst_ref=r2.at[it, side, d - 1, slot],
            send_sem=s2_send.at[0], recv_sem=s2_recv.at[slot],
            device_id=along(1 - side, d), device_id_type=MESH,
        )

    def on_line(side, chunk):
        return chunk * SIDE + y if side == 0 else x * SIDE + chunk

    def gather_copy(it, side, d, chunk):
        block = images.at[it, on_line(side, chunk), half(side)]
        return pltpu.make_async_remote_copy(
            src_ref=block, dst_ref=block, send_sem=g_send.at[0], recv_sem=g_recv.at[chunk],
            device_id=along(side, d), device_id_type=MESH,
        )

    def wait_for(ref, sem):
        pltpu.make_async_copy(ref, ref, sem).wait()

    def small_copy(it, side, d):
        return pltpu.make_async_remote_copy(
            src_ref=small.at[it, side], dst_ref=small_in.at[it, side, d - 1],
            send_sem=small_send.at[side], recv_sem=small_recv.at[side],
            device_id=along(side, d), device_id_type=MESH,
        )

    def small_start(it, side, value):
        small[it, side] = value
        for d in (2, 1, 3):
            small_copy(it, side, d).start()

    def small_sum(it, side):
        wait_for(small_in.at[it, side], small_recv.at[side])
        return small[it, side] + small_in[it, side, 0] + small_in[it, side, 1] + small_in[it, side, 2]

    def small_end(it):
        for side in (0, 1):
            wait_for(small_in.at[it, side], small_send.at[side])

    def norm_copy(dx, dy):
        return pltpu.make_async_remote_copy(
            src_ref=norm_out, dst_ref=norm_in.at[dx * SIDE + dy - 1], send_sem=norm_send.at[0], recv_sem=norm_recv.at[0],
            device_id=at(dx, dy), device_id_type=MESH,
        )

    def left_half(t, v):
        left = jnp.concatenate([lcat[w, target[w * NS + t]] for w in range(SLOTS)], axis=0)
        high, low = split(product(left, doubled(v)))
        for w in range(SLOTS):
            part = slice(w * BK, (w + 1) * BK)
            inner[w, t] = jnp.concatenate([high[part], low[part]], axis=0)

    def right_half(s, scale):
        left = jnp.concatenate([inner[w, source[w * NS + s]] for w in range(SLOTS)], axis=1)
        both = lax.dot_general(left, rcat[s], (((1,), (1,)), ((), ())), preferred_element_type=F32)
        return (both[:BK, :BK] + both[:BK, BK:] + both[BK:, :BK] + both[BK:, BK:]) * scale

    for it in range(ITERS):
        if it == 0:
            def begin(t, carry):
                v = waves[0, t] * scale
                waves[0, t] = v
                left_half(t, v)
                return carry

            lax.fori_loop(0, NS, begin, 0, unroll=4)
            scale = jnp.float32(1)
            for w in range(SLOTS):
                load_r[w].wait()

                def set_right(s, carry):
                    high, low = split(stage_r[w, s] * mask[w * NS + s])
                    rcat[s, 0:BK, w * BK:(w + 1) * BK] = high
                    rcat[s, BK:2 * BK, w * BK:(w + 1) * BK] = low
                    return carry

                lax.fori_loop(0, NS, set_right, 0, unroll=2)
        else:
            theta = jnp.sum(small_sum(it - 1, 1)) / ENTRIES

            squares = zero
            for chunk in range(SIDE):
                wait_for(r1.at[it - 1, :, :, chunk], g_recv.at[chunk])
                blocks = [sx * SIDE + sy for sx, sy in last_shell(chunk)]
                for t in blocks:
                    wave = waves[it - 1, t] * scale
                    wave = wave - step_size * (images[it - 1, t] - theta * wave)
                    left_half(t, wave)
                    waves[it, t] = wave
                    squares = squares + fold(wave * wave)
            scale = scale_from(squares)
            wait_for(r1.at[it - 1], g_send.at[0])
            small_end(it - 1)

        total = zero
        for chunk in range(SIDE):
            blocks = [sx * SIDE + sy for sx, sy in first_shell(chunk)]
            for s in blocks:
                block = right_half(s, scale)
                image_parts[it, s] = block
                total = total + fold(block * waves[it, s])
            for d in (2, 1, 3):
                for side in (0, 1):
                    s1_copy(it, side, d, chunk).start()
        small_start(it, 0, total * scale)
        if it == 0:
            first_maps()
        else:
            more_maps((3, 4) if it == 1 else (6, 7))

        for chunk in range(SIDE):
            wait_for(r1.at[it, :, :, chunk], s1_recv.at[chunk])
            for side in (0, 1):
                block = image_parts[it, on_line(side, chunk), half(side)]
                for e in range(SIDE - 1):
                    block = block + r1[it, side, e, chunk]
                p2[it, side, chunk] = block
                if it + 1 < ITERS:
                    for d in (2, 1, 3):
                        s2_copy(it, side, d, chunk, chunk).start()
                else:
                    d = (chunk - (x if side == 0 else y) + SIDE) % SIDE

                    @pl.when(d != 0)
                    def _():
                        s2_copy(it, side, d, chunk, 0).start()

        small_start(it, 1, small_sum(it, 0))
        if it + 1 < ITERS:
            more_maps((2,) if it == 0 else (5,))

        def sum_of(side, chunk, slot):
            block = p2[it, side, chunk]
            for e in range(SIDE - 1):
                block = block + r2[it, side, e, slot]
            return block

        if it + 1 < ITERS:
            for chunk in range(SIDE):
                wait_for(r2.at[it, :, :, chunk], s2_recv.at[chunk])
                for side in (0, 1):
                    images[it, on_line(side, chunk), half(side)] = sum_of(side, chunk, chunk)
                    for d in (2, 1, 3):
                        gather_copy(it, side, d, chunk).start()
            wait_for(r2.at[it], s2_send.at[0])
        else:
            wait_for(r2.at[it, :, :, 0], s2_recv.at[0])
            image = jnp.concatenate([sum_of(0, x, 0), sum_of(1, y, 0)], axis=0)
            theta = jnp.sum(small_sum(it, 1)) / ENTRIES
            wave = waves[it, own] * scale
            wave = wave - step_size * (image - theta * wave)
            norm_out[...] = fold(wave * wave)
            for dx, dy in others:
                norm_copy(dx, dy).start()
            wait_for(r2.at[it, :, :, 0], s2_send.at[0])
        wait_for(r1.at[it], s1_send.at[0])

    energy = product(beside(wave.T), doubled(image))

    @pl.when(core == 0)
    def _():
        e_out[...] = energy
        core_copy(e_out, e_in, 1).start()

    @pl.when(core == 1)
    def _():
        core_copy(e_out, e_in, 1).wait_recv()
        n_out[...] = product(tt[...], doubled(product(beside(e_in[...]), tdup[...])))

    squares = norm_out[...]
    wait_for(norm_in, norm_recv.at[0])
    for slot in range(NS - 1):
        squares = squares + norm_in[slot]
    scale = scale_from(squares)
    energy_scale = scale / BK

    @pl.when(core == 0)
    def _():
        c_out[...] = jnp.full((8, BK), energy_scale, F32)
        core_copy(c_out, c_in, 2).start()

    out[0] = wave * scale

    @pl.when(core == 1)
    def _():
        core_copy(c_out, c_in, 2).wait_recv()
        lower = n_out[...] * c_in[0:1, 0:1]
        f_out[...] = energy * energy_scale + lower
        for d in range(CHIPS - 1, 0, -1):
            @pl.when(z + d < CHIPS)
            def _():
                up_copy(f_out, f_in, f_send, f_recv, d).start()

        out[1] = lower
        n_out[...] = jnp.zeros((BK, BK), F32)
        for d in range(1, CHIPS):
            @pl.when(z >= d)
            def _():
                up_copy(f_out, f_in, f_send, f_recv, d).wait_recv()
                n_out[...] += product(wt[d - 1], doubled(product(beside(f_in[d - 1]), wdup[d - 1])))

        core_copy(n_out, n_in, 3).start()
        out[1] += product(tt[...], doubled(product(beside(n_out[...]), tdup[...])))
        for d in range(1, CHIPS):
            @pl.when(z + d < CHIPS)
            def _():
                up_copy(f_out, f_in, f_send, f_recv, d).wait_send()

            if d < CHIPS - 1:
                @pl.when((z >= 1) & (z + d < CHIPS))
                def _():
                    up_copy(pair_out, pair_in, pair_send, pair_recv, d).wait_send()

        core_copy(n_out, n_in, 3).wait_send()

    @pl.when(core == 0)
    def _():
        core_copy(t_out, t_in, 0).wait_send()
        core_copy(e_out, e_in, 1).wait_send()
        core_copy(c_out, c_in, 2).wait_send()
        core_copy(n_out, n_in, 3).wait_recv()
        out[1] = n_in[...]

    wait_for(norm_in, norm_send.at[0])
    small_end(ITERS - 1)


def shards(wave_in, env_left, env_right, sector_charge, term_charge, term_live, transfer):
    vmem = pl.BlockSpec(memory_space=pltpu.VMEM)
    hbm = pl.BlockSpec(memory_space=pl.ANY)
    dma = pltpu.SemaphoreType.DMA
    square = pltpu.VMEM((BK, BK), F32)
    tile = pltpu.VMEM((8, BK), F32)
    both = pl.pallas_call(
        kernel,
        out_shape=jax.ShapeDtypeStruct((2, BK, BK), F32),
        in_specs=[hbm, hbm, hbm, hbm, hbm, hbm, hbm],
        out_specs=vmem,
        scratch_shapes=[
            pltpu.SMEM((2, NS), jnp.int32),
            pltpu.SMEM((2, SLOTS), jnp.int32),
            pltpu.SMEM((SLOTS,), jnp.int32),
            pltpu.SMEM((NS,), jnp.int32),
            pltpu.SMEM((NS,), jnp.int32),
            pltpu.SMEM((SLOTS * NS,), jnp.int32),
            pltpu.SMEM((SLOTS * NS,), jnp.int32),
            pltpu.SMEM((SLOTS * NS,), F32),
            pltpu.VMEM((SLOTS, NS, BK, BK), F32),
            pltpu.VMEM((SLOTS, NS, BK, BK), F32),
            square,
            pltpu.VMEM((SLOTS, NS, BK, 2 * BK), BF16),
            pltpu.VMEM((NS, 2 * BK, SLOTS * BK), BF16),
            pltpu.VMEM((SLOTS, NS, 2 * BK, BK), BF16),
            pltpu.VMEM((ITERS, NS, BK, BK), F32),
            pltpu.VMEM((ITERS, NS, BK, BK), F32),
            pltpu.VMEM((ITERS - 1, NS, BK, BK), F32),
            pltpu.VMEM((ITERS, 2, SIDE - 1, SIDE, HALF, BK), F32),
            pltpu.VMEM((ITERS, 2, SIDE, HALF, BK), F32),
            pltpu.VMEM((ITERS, 2, SIDE - 1, SIDE, HALF, BK), F32),
            pltpu.VMEM((ITERS, 2, 8, BK), F32),
            pltpu.VMEM((ITERS, 2, SIDE - 1, 8, BK), F32),
            tile,
            pltpu.VMEM((NS - 1, 8, BK), F32),
            square,
            square,
            square,
            pltpu.VMEM((CHIPS - 2, BK, BK), F32),
            pltpu.VMEM((2 * BK, 2 * BK), BF16),
            pltpu.VMEM((BK, 2 * BK), BF16),
            pltpu.VMEM((CHIPS - 1, 2 * BK, 2 * BK), BF16),
            pltpu.VMEM((CHIPS - 1, BK, 2 * BK), BF16),
            square,
            square,
            tile,
            tile,
            square,
            pltpu.VMEM((CHIPS - 1, BK, BK), F32),
            square,
            square,
            dma((5 + 2 * SLOTS,)),
            dma((1,)),
            dma((SIDE,)),
            dma((1,)),
            dma((SIDE,)),
            dma((1,)),
            dma((SIDE,)),
            dma((2,)),
            dma((2,)),
            dma((1,)),
            dma((1,)),
            dma((4,)),
            dma((4,)),
            dma((CHIPS - 2,)),
            dma((CHIPS - 2,)),
            dma((CHIPS - 1,)),
            dma((CHIPS - 1,)),
        ],
        compiler_params=pltpu.CompilerParams(
            collective_id=0, has_side_effects=True, vmem_limit_bytes=56 * 1024 * 1024
        ),
    )(sector_charge.T, term_charge.T, term_live, wave_in, env_left, env_right, transfer)
    block = (1, 1, BK, BK)
    return both[0].reshape(block), both[1].reshape(block)


def solution(mesh):
    in_specs = (
        P("seg", None, None, None),
        P("seg", "term", None, None, None),
        P("seg", "term", None, None, None),
        P(),
        P("term", None),
        P("term"),
        P("seg", None, None, None),
    )
    out_specs = (P("seg", "term", None, None), P("seg", "term", None, None))
    return jax.shard_map(shards, mesh=mesh, in_specs=in_specs, out_specs=out_specs, check_vma=False)
```

```python
import functools

import jax
import jax.numpy as jnp
from jax import lax
from jax.experimental import pallas as pl
from jax.experimental.pallas import tpu as pltpu
from jax.sharding import PartitionSpec as P

ITERS = 3
SIDE = 4
CHARGES = 4
BK = 128
HALF = 64
NS = 16
SLOTS = 4
NSEG = 16
EARLY = 8
CHIPS = NSEG // 2
ENTRIES = float(NS * BK * BK)
mean_eps = 1e-06
step_size = 0.5

F32 = jnp.float32
BF16 = jnp.bfloat16
MESH = pl.DeviceIdType.MESH


def split(x):
    high = x.astype(BF16)
    low = (x - high.astype(F32)).astype(BF16)
    return high, low


def beside(x):
    return jnp.concatenate(split(x), axis=1)


def doubled(x):
    row = beside(x)
    return jnp.concatenate([row, row], axis=0)


def product(left, right):
    both = jnp.dot(left, right, preferred_element_type=F32)
    return both[:, :BK] + both[:, BK:]


def fold(x):
    return jnp.sum(x.reshape(x.shape[0] // 8, 8, x.shape[1]), axis=0)


def first_shell(r):
    return [(r, k) for k in range(r, SIDE)] + [(k, r) for k in range(r + 1, SIDE)]


def last_shell(r):
    return [(r, k) for k in range(r)] + [(k, r) for k in range(r)] + [(r, r)]


def kernel(
    sector_hbm, term_hbm, live_hbm, wave_hbm, left_hbm, right_hbm, transfer_hbm,
    out,
    sector_ref, term_ref, live_ref, code, place, source, target, mask,
    stage_l, stage_r, stage_t, lcat, rcat, inner, waves, image_parts, images,
    r1, p2, r2, small, small_in, norm_out, norm_in,
    t_out, t_in, pair_out, pair_in, tdup, tt, wdup, wt, e_out, e_in, lower_in, f_out, f_in, n_out, n_in,
    load_sem, s1_send, s1_recv, s2_send, s2_recv, g_send, g_recv,
    small_send, small_recv, norm_send, norm_recv, lower_send, lower_recv, ready, core_send, core_recv, pair_send, pair_recv, f_send, f_recv,
):
    seg = lax.axis_index("seg")
    own = lax.axis_index("term")
    x, y = own // SIDE, own % SIDE
    z, core = seg // 2, seg % 2

    def at(dx, dy):
        return (seg, ((x + dx) % SIDE) * SIDE + (y + dy) % SIDE)

    def beyond(dx, dy):
        return (seg + 1 - 2 * core, at(dx, dy)[1])

    other_core = beyond(0, 0)

    load_w = pltpu.make_async_copy(wave_hbm.at[0], waves.at[0], load_sem.at[0])
    load_t = pltpu.make_async_copy(transfer_hbm.at[0, own], stage_t, load_sem.at[1])
    load_i = [
        pltpu.make_async_copy(sector_hbm, sector_ref, load_sem.at[10]),
        pltpu.make_async_copy(term_hbm, term_ref, load_sem.at[11]),
        pltpu.make_async_copy(live_hbm, live_ref, load_sem.at[12]),
    ]
    for load in load_i:
        load.start()
    load_w.start()
    load_t.start()
    load_l = [pltpu.make_async_copy(left_hbm.at[0, w], stage_l.at[w], load_sem.at[2 + w]) for w in range(SLOTS)]
    load_r = [pltpu.make_async_copy(right_hbm.at[0, w], stage_r.at[w], load_sem.at[6 + w]) for w in range(SLOTS)]
    for load in load_l + load_r:
        load.start()
    barrier = pltpu.get_barrier_semaphore()
    others = [(dx, dy) for dx in (2, 1, 3, 0) for dy in (2, 1, 3, 0) if (dx, dy) != (0, 0)]
    for dx, dy in others:
        pl.semaphore_signal(barrier, inc=1, device_id=at(dx, dy), device_id_type=MESH)
    pl.semaphore_signal(barrier, inc=1, device_id=other_core, device_id_type=MESH)

    @pl.when(core == 1)
    def _():
        for dx, dy in others:
            pl.semaphore_signal(barrier, inc=1, device_id=beyond(dx, dy), device_id_type=MESH)

    for d in range(1, CHIPS):
        @pl.when(z + d < CHIPS)
        def _():
            pl.semaphore_signal(barrier, inc=1, device_id=((seg + 2 * d) % NSEG, own), device_id_type=MESH)

    for load in load_i:
        load.wait()
    for s in range(NS):
        code[s] = sector_ref[0, s] * CHARGES + sector_ref[1, s]

    def sector_at(up, down):
        inside = (up >= 0) & (up < CHARGES) & (down >= 0) & (down < CHARGES)
        return inside, place[jnp.where(inside, up * CHARGES + down, 0)]

    def look_up(w, s):
        up, down = sector_ref[0, s], sector_ref[1, s]
        up_change, down_change = term_ref[0, w], term_ref[1, w]
        inside, found = sector_at(up - up_change, down - down_change)
        source[w * NS + s] = found
        mask[w * NS + s] = jnp.where(inside, live_ref[w].astype(F32), jnp.float32(0))
        target[w * NS + s] = sector_at(up + up_change, down + down_change)[1]

    load_w.wait()

    def add_square(t, total):
        found = jnp.int32(0)
        for s in range(NS):
            found = jnp.where(code[s] == t, jnp.int32(s), found)
        place[t] = found
        v = waves[0, t]
        return total + fold(v * v)

    def scale_from(squares):
        return lax.rsqrt(jnp.sum(squares) / ENTRIES + mean_eps)

    zero = jnp.zeros((8, BK), F32)
    squares = lax.fori_loop(0, NS, add_square, zero, unroll=2)
    scale = scale_from(squares)

    for w in range(SLOTS):
        load_l[w].wait()

        def set_left(s, carry):
            lcat[w, s] = beside(stage_l[w, s])
            look_up(w, s)
            return carry

        lax.fori_loop(0, NS, set_left, 0, unroll=2)

    def core_copy(src, dst, k):
        return pltpu.make_async_remote_copy(
            src_ref=src, dst_ref=dst, send_sem=core_send.at[k], recv_sem=core_recv.at[k],
            device_id=other_core, device_id_type=MESH,
        )

    def up_copy(src, dst, send, recv, d):
        return pltpu.make_async_remote_copy(
            src_ref=src, dst_ref=dst.at[d - 1], send_sem=send.at[d - 1], recv_sem=recv.at[d - 1],
            device_id=((seg + 2 * d) % NSEG, own), device_id_type=MESH,
        )

    def set_map(d, value):
        wdup[d - 1] = doubled(value)
        wt[d - 1] = beside(value.T)

    def first_maps():
        @pl.when(core == 1)
        def _():
            own_map = t_out[...]
            tdup[...] = doubled(own_map)
            tt[...] = beside(own_map.T)
            @pl.when(z < CHIPS - 1)
            def _():
                pl.semaphore_wait(ready, CHIPS - 1 - z)

            core_copy(t_out, t_in, 0).wait_recv()
            lower_map = t_in[...]
            set_map(1, lower_map)
            pair_out[...] = product(beside(lower_map), tdup[...])
            for d in range(1, CHIPS - 1):
                @pl.when((z >= 1) & (z + d < CHIPS))
                def _():
                    up_copy(pair_out, pair_in, pair_send, pair_recv, d).start()

    def more_maps(which):
        for d in which:
            @pl.when((core == 1) & (z >= d))
            def _():
                up_copy(pair_out, pair_in, pair_send, pair_recv, d - 1).wait_recv()
                set_map(d, product(beside(pair_in[d - 2]), wdup[d - 2]))

    def half(side):
        return pl.ds(side * HALF, HALF)

    def along(side, d):
        return at(0, d) if side == 0 else at(d, 0)

    def s1_copy(it, side, d, chunk):
        sector = chunk * SIDE + (y + d) % SIDE if side == 0 else ((x + d) % SIDE) * SIDE + chunk
        return pltpu.make_async_remote_copy(
            src_ref=image_parts.at[it, sector, half(side)], dst_ref=r1.at[it, side, d - 1, chunk],
            send_sem=s1_send.at[0], recv_sem=s1_recv.at[chunk],
            device_id=along(side, d), device_id_type=MESH,
        )

    def s2_copy(it, side, d, chunk, slot):
        return pltpu.make_async_remote_copy(
            src_ref=p2.at[it, side, chunk], dst_ref=r2.at[it, side, d - 1, slot],
            send_sem=s2_send.at[0], recv_sem=s2_recv.at[slot],
            device_id=along(1 - side, d), device_id_type=MESH,
        )

    def on_line(side, chunk):
        return chunk * SIDE + y if side == 0 else x * SIDE + chunk

    def gather_copy(it, side, d, chunk):
        block = images.at[it, on_line(side, chunk), half(side)]
        return pltpu.make_async_remote_copy(
            src_ref=block, dst_ref=block, send_sem=g_send.at[0], recv_sem=g_recv.at[chunk],
            device_id=along(side, d), device_id_type=MESH,
        )

    def wait_for(ref, sem):
        pltpu.make_async_copy(ref, ref, sem).wait()

    def small_copy(it, side, d):
        return pltpu.make_async_remote_copy(
            src_ref=small.at[it, side], dst_ref=small_in.at[it, side, d - 1],
            send_sem=small_send.at[side], recv_sem=small_recv.at[side],
            device_id=along(side, d), device_id_type=MESH,
        )

    def small_start(it, side, value):
        small[it, side] = value
        for d in (2, 1, 3):
            small_copy(it, side, d).start()

    def small_sum(it, side):
        wait_for(small_in.at[it, side], small_recv.at[side])
        return small[it, side] + small_in[it, side, 0] + small_in[it, side, 1] + small_in[it, side, 2]

    def small_end(it):
        for side in (0, 1):
            wait_for(small_in.at[it, side], small_send.at[side])

    def norm_copy(dx, dy):
        return pltpu.make_async_remote_copy(
            src_ref=norm_out, dst_ref=norm_in.at[dx * SIDE + dy - 1], send_sem=norm_send.at[0], recv_sem=norm_recv.at[0],
            device_id=at(dx, dy), device_id_type=MESH,
        )

    def lower_copy(dx, dy):
        return pltpu.make_async_remote_copy(
            src_ref=norm_out, dst_ref=lower_in.at[dx * SIDE + dy], send_sem=lower_send.at[0], recv_sem=lower_recv.at[0],
            device_id=beyond(dx, dy), device_id_type=MESH,
        )

    def left_half(t, v):
        left = jnp.concatenate([lcat[w, target[w * NS + t]] for w in range(SLOTS)], axis=0)
        high, low = split(product(left, doubled(v)))
        for w in range(SLOTS):
            part = slice(w * BK, (w + 1) * BK)
            inner[w, t] = jnp.concatenate([high[part], low[part]], axis=0)

    def right_half(s, scale):
        left = jnp.concatenate([inner[w, source[w * NS + s]] for w in range(SLOTS)], axis=1)
        both = lax.dot_general(left, rcat[s], (((1,), (1,)), ((), ())), preferred_element_type=F32)
        return (both[:BK, :BK] + both[:BK, BK:] + both[BK:, :BK] + both[BK:, BK:]) * scale

    for it in range(ITERS):
        if it == 0:
            def begin(t):
                v = waves[0, t] * scale
                waves[0, t] = v
                left_half(t, v)

            def set_right(s):
                for w in range(SLOTS):
                    high, low = split(stage_r[w, s] * mask[w * NS + s])
                    rcat[s, 0:BK, w * BK:(w + 1) * BK] = high
                    rcat[s, BK:2 * BK, w * BK:(w + 1) * BK] = low

            def begin_early(p, carry):
                begin(2 * p)
                begin(2 * p + 1)
                return carry

            def begin_late(p, carry):
                begin(EARLY + p)
                for j in range(NS // (NS - EARLY)):
                    set_right(NS // (NS - EARLY) * p + j)
                return carry

            lax.fori_loop(0, EARLY // 2, begin_early, 0)
            for load in load_r:
                load.wait()
            lax.fori_loop(0, NS - EARLY, begin_late, 0, unroll=2)
            scale = jnp.float32(1)

            load_t.wait()
            rows = lax.broadcasted_iota(jnp.int32, (BK, BK), 0)
            columns = lax.broadcasted_iota(jnp.int32, (BK, BK), 1)
            t_out[...] = stage_t[...] + jnp.where(rows == columns, jnp.float32(1), jnp.float32(0))
            pl.semaphore_wait(barrier, len(others) + 1 + z + (1 - core) * len(others))

            @pl.when(core == 0)
            def _():
                core_copy(t_out, t_in, 0).start()

            @pl.when(core == 1)
            def _():
                for d in range(1, CHIPS):
                    @pl.when(z >= d)
                    def _():
                        pl.semaphore_signal(
                            ready, inc=1, device_id=((seg - 2 * d + NSEG) % NSEG, own), device_id_type=MESH
                        )
        else:
            theta = jnp.sum(small_sum(it - 1, 1)) / ENTRIES

            squares = zero
            for chunk in range(SIDE):
                wait_for(r1.at[it - 1, :, :, chunk], g_recv.at[chunk])
                blocks = [sx * SIDE + sy for sx, sy in last_shell(chunk)]
                for t in blocks:
                    wave = waves[it - 1, t] * scale
                    wave = wave - step_size * (images[it - 1, t] - theta * wave)
                    left_half(t, wave)
                    waves[it, t] = wave
                    squares = squares + fold(wave * wave)
            scale = scale_from(squares)
            wait_for(r1.at[it - 1], g_send.at[0])
            small_end(it - 1)

        total = zero
        for chunk in range(SIDE):
            blocks = [sx * SIDE + sy for sx, sy in first_shell(chunk)]
            for s in blocks:
                block = right_half(s, scale)
                image_parts[it, s] = block
                total = total + fold(block * waves[it, s])
            for d in (2, 1, 3):
                for side in (0, 1):
                    s1_copy(it, side, d, chunk).start()
        small_start(it, 0, total * scale)
        if it == 0:
            first_maps()
        else:
            more_maps((3, 4) if it == 1 else (6, 7))

        for chunk in range(SIDE):
            wait_for(r1.at[it, :, :, chunk], s1_recv.at[chunk])
            for side in (0, 1):
                block = image_parts[it, on_line(side, chunk), half(side)]
                for e in range(SIDE - 1):
                    block = block + r1[it, side, e, chunk]
                p2[it, side, chunk] = block
                if it + 1 < ITERS:
                    for d in (2, 1, 3):
                        s2_copy(it, side, d, chunk, chunk).start()
                else:
                    d = (chunk - (x if side == 0 else y) + SIDE) % SIDE

                    @pl.when(d != 0)
                    def _():
                        s2_copy(it, side, d, chunk, 0).start()

        small_start(it, 1, small_sum(it, 0))
        if it + 1 < ITERS:
            more_maps((2,) if it == 0 else (5,))

        def sum_of(side, chunk, slot):
            block = p2[it, side, chunk]
            for e in range(SIDE - 1):
                block = block + r2[it, side, e, slot]
            return block

        if it + 1 < ITERS:
            for chunk in range(SIDE):
                wait_for(r2.at[it, :, :, chunk], s2_recv.at[chunk])
                for side in (0, 1):
                    images[it, on_line(side, chunk), half(side)] = sum_of(side, chunk, chunk)
                    for d in (2, 1, 3):
                        gather_copy(it, side, d, chunk).start()
            wait_for(r2.at[it], s2_send.at[0])
        else:
            wait_for(r2.at[it, :, :, 0], s2_recv.at[0])
            image = jnp.concatenate([sum_of(0, x, 0), sum_of(1, y, 0)], axis=0)
            theta = jnp.sum(small_sum(it, 1)) / ENTRIES
            wave = waves[it, own] * scale
            wave = wave - step_size * (image - theta * wave)
            norm_out[...] = fold(wave * wave)
            for dx, dy in others:
                norm_copy(dx, dy).start()

            @pl.when(core == 0)
            def _():
                for dx, dy in others + [(0, 0)]:
                    lower_copy(dx, dy).start()

            wait_for(r2.at[it, :, :, 0], s2_send.at[0])
        wait_for(r1.at[it], s1_send.at[0])

    energy = product(beside(wave.T), doubled(image))

    @pl.when(core == 0)
    def _():
        e_out[...] = energy
        core_copy(e_out, e_in, 1).start()

    @pl.when(core == 1)
    def _():
        core_copy(e_out, e_in, 1).wait_recv()
        n_out[...] = product(tt[...], doubled(product(beside(e_in[...]), tdup[...])))

    squares = norm_out[...]
    wait_for(norm_in, norm_recv.at[0])
    for slot in range(NS - 1):
        squares = squares + norm_in[slot]
    scale = scale_from(squares)
    energy_scale = scale / BK

    out[0] = wave * scale

    @pl.when(core == 1)
    def _():
        wait_for(lower_in, lower_recv.at[0])
        lower_squares = lower_in[0]
        for slot in range(1, NS):
            lower_squares = lower_squares + lower_in[slot]
        lower = n_out[...] * (scale_from(lower_squares) / BK)
        f_out[...] = energy * energy_scale + lower
        for d in range(CHIPS - 1, 0, -1):
            @pl.when(z + d < CHIPS)
            def _():
                up_copy(f_out, f_in, f_send, f_recv, d).start()

        out[1] = lower
        n_out[...] = jnp.zeros((BK, BK), F32)
        for d in range(1, CHIPS):
            @pl.when(z >= d)
            def _():
                up_copy(f_out, f_in, f_send, f_recv, d).wait_recv()
                n_out[...] += product(wt[d - 1], doubled(product(beside(f_in[d - 1]), wdup[d - 1])))

        core_copy(n_out, n_in, 2).start()
        out[1] += product(tt[...], doubled(product(beside(n_out[...]), tdup[...])))
        for d in range(1, CHIPS):
            @pl.when(z + d < CHIPS)
            def _():
                up_copy(f_out, f_in, f_send, f_recv, d).wait_send()

            if d < CHIPS - 1:
                @pl.when((z >= 1) & (z + d < CHIPS))
                def _():
                    up_copy(pair_out, pair_in, pair_send, pair_recv, d).wait_send()

        core_copy(n_out, n_in, 2).wait_send()

    @pl.when(core == 0)
    def _():
        core_copy(t_out, t_in, 0).wait_send()
        core_copy(e_out, e_in, 1).wait_send()
        wait_for(lower_in, lower_send.at[0])
        core_copy(n_out, n_in, 2).wait_recv()
        out[1] = n_in[...]

    wait_for(norm_in, norm_send.at[0])
    small_end(ITERS - 1)


def shards(wave_in, env_left, env_right, sector_charge, term_charge, term_live, transfer):
    vmem = pl.BlockSpec(memory_space=pltpu.VMEM)
    hbm = pl.BlockSpec(memory_space=pl.ANY)
    dma = pltpu.SemaphoreType.DMA
    square = pltpu.VMEM((BK, BK), F32)
    tile = pltpu.VMEM((8, BK), F32)
    both = pl.pallas_call(
        kernel,
        out_shape=jax.ShapeDtypeStruct((2, BK, BK), F32),
        in_specs=[hbm, hbm, hbm, hbm, hbm, hbm, hbm],
        out_specs=vmem,
        scratch_shapes=[
            pltpu.SMEM((2, NS), jnp.int32),
            pltpu.SMEM((2, SLOTS), jnp.int32),
            pltpu.SMEM((SLOTS,), jnp.int32),
            pltpu.SMEM((NS,), jnp.int32),
            pltpu.SMEM((NS,), jnp.int32),
            pltpu.SMEM((SLOTS * NS,), jnp.int32),
            pltpu.SMEM((SLOTS * NS,), jnp.int32),
            pltpu.SMEM((SLOTS * NS,), F32),
            pltpu.VMEM((SLOTS, NS, BK, BK), F32),
            pltpu.VMEM((SLOTS, NS, BK, BK), F32),
            square,
            pltpu.VMEM((SLOTS, NS, BK, 2 * BK), BF16),
            pltpu.VMEM((NS, 2 * BK, SLOTS * BK), BF16),
            pltpu.VMEM((SLOTS, NS, 2 * BK, BK), BF16),
            pltpu.VMEM((ITERS, NS, BK, BK), F32),
            pltpu.VMEM((ITERS, NS, BK, BK), F32),
            pltpu.VMEM((ITERS - 1, NS, BK, BK), F32),
            pltpu.VMEM((ITERS, 2, SIDE - 1, SIDE, HALF, BK), F32),
            pltpu.VMEM((ITERS, 2, SIDE, HALF, BK), F32),
            pltpu.VMEM((ITERS, 2, SIDE - 1, SIDE, HALF, BK), F32),
            pltpu.VMEM((ITERS, 2, 8, BK), F32),
            pltpu.VMEM((ITERS, 2, SIDE - 1, 8, BK), F32),
            tile,
            pltpu.VMEM((NS - 1, 8, BK), F32),
            square,
            square,
            square,
            pltpu.VMEM((CHIPS - 2, BK, BK), F32),
            pltpu.VMEM((2 * BK, 2 * BK), BF16),
            pltpu.VMEM((BK, 2 * BK), BF16),
            pltpu.VMEM((CHIPS - 1, 2 * BK, 2 * BK), BF16),
            pltpu.VMEM((CHIPS - 1, BK, 2 * BK), BF16),
            square,
            square,
            pltpu.VMEM((NS, 8, BK), F32),
            square,
            pltpu.VMEM((CHIPS - 1, BK, BK), F32),
            square,
            square,
            dma((5 + 2 * SLOTS,)),
            dma((1,)),
            dma((SIDE,)),
            dma((1,)),
            dma((SIDE,)),
            dma((1,)),
            dma((SIDE,)),
            dma((2,)),
            dma((2,)),
            dma((1,)),
            dma((1,)),
            dma((1,)),
            dma((1,)),
            pltpu.SemaphoreType.REGULAR,
            dma((3,)),
            dma((3,)),
            dma((CHIPS - 2,)),
            dma((CHIPS - 2,)),
            dma((CHIPS - 1,)),
            dma((CHIPS - 1,)),
        ],
        compiler_params=pltpu.CompilerParams(
            collective_id=0, has_side_effects=True, vmem_limit_bytes=56 * 1024 * 1024
        ),
    )(sector_charge.T, term_charge.T, term_live, wave_in, env_left, env_right, transfer)
    block = (1, 1, BK, BK)
    return both[0].reshape(block), both[1].reshape(block)


def solution(mesh):
    in_specs = (
        P("seg", None, None, None),
        P("seg", "term", None, None, None),
        P("seg", "term", None, None, None),
        P(),
        P("term", None),
        P("term"),
        P("seg", None, None, None),
    )
    out_specs = (P("seg", "term", None, None), P("seg", "term", None, None))
    return jax.shard_map(shards, mesh=mesh, in_specs=in_specs, out_specs=out_specs, check_vma=False)
```

```python
import functools

import jax
import jax.numpy as jnp
from jax import lax
from jax.experimental import pallas as pl
from jax.experimental.pallas import tpu as pltpu
from jax.sharding import PartitionSpec as P

ITERS = 3
SIDE = 4
CHARGES = 4
BK = 128
HALF = 64
NS = 16
SLOTS = 4
NSEG = 16
EARLY = 8
CHIPS = NSEG // 2
ENTRIES = float(NS * BK * BK)
mean_eps = 1e-06
step_size = 0.5

F32 = jnp.float32
BF16 = jnp.bfloat16
MESH = pl.DeviceIdType.MESH


def split(x):
    high = x.astype(BF16)
    low = (x - high.astype(F32)).astype(BF16)
    return high, low


def beside(x):
    return jnp.concatenate(split(x), axis=1)


def doubled(x):
    row = beside(x)
    return jnp.concatenate([row, row], axis=0)


def product(left, right):
    both = jnp.dot(left, right, preferred_element_type=F32)
    return both[:, :BK] + both[:, BK:]


def fold(x):
    return jnp.sum(x.reshape(x.shape[0] // 8, 8, x.shape[1]), axis=0)


def first_shell(r):
    return [(r, k) for k in range(r, SIDE)] + [(k, r) for k in range(r + 1, SIDE)]


def last_shell(r):
    return [(r, k) for k in range(r)] + [(k, r) for k in range(r)] + [(r, r)]


def kernel(
    sector_hbm, term_hbm, live_hbm, wave_hbm, left_hbm, right_hbm, transfer_hbm,
    out,
    sector_ref, term_ref, live_ref, code, place, source, target, mask,
    stage_l, stage_r, stage_t, lcat, rcat, inner, waves, image_parts, images,
    r1, p2, r2, small, small_in, norm_out, norm_in,
    t_out, t_in, pair_out, pair_in, tdup, tt, wdup, wt, e_out, e_in, lower_in, f_out, f_in, n_out, n_in,
    load_sem, s1_send, s1_recv, s2_send, s2_recv, g_send, g_recv,
    small_send, small_recv, norm_send, norm_recv, lower_send, lower_recv, ready, core_send, core_recv, pair_send, pair_recv, f_send, f_recv,
):
    seg = lax.axis_index("seg")
    own = lax.axis_index("term")
    x, y = own // SIDE, own % SIDE
    z, core = seg // 2, seg % 2

    def at(dx, dy):
        return (seg, ((x + dx) % SIDE) * SIDE + (y + dy) % SIDE)

    def beyond(dx, dy):
        return (seg + 1 - 2 * core, at(dx, dy)[1])

    other_core = beyond(0, 0)

    load_w = pltpu.make_async_copy(wave_hbm.at[0], waves.at[0], load_sem.at[0])
    load_t = pltpu.make_async_copy(transfer_hbm.at[0, own], stage_t, load_sem.at[1])
    load_i = [
        pltpu.make_async_copy(sector_hbm, sector_ref, load_sem.at[10]),
        pltpu.make_async_copy(term_hbm, term_ref, load_sem.at[11]),
        pltpu.make_async_copy(live_hbm, live_ref, load_sem.at[12]),
    ]
    for load in load_i:
        load.start()
    load_w.start()
    load_t.start()
    load_l = [pltpu.make_async_copy(left_hbm.at[0, w], stage_l.at[w], load_sem.at[2 + w]) for w in range(SLOTS)]
    load_r = [pltpu.make_async_copy(right_hbm.at[0, w], stage_r.at[w], load_sem.at[6 + w]) for w in range(SLOTS)]
    for load in load_l + load_r:
        load.start()
    barrier = pltpu.get_barrier_semaphore()
    others = [(dx, dy) for dx in (2, 1, 3, 0) for dy in (2, 1, 3, 0) if (dx, dy) != (0, 0)]
    for dx, dy in others:
        pl.semaphore_signal(barrier, inc=1, device_id=at(dx, dy), device_id_type=MESH)
    pl.semaphore_signal(barrier, inc=1, device_id=other_core, device_id_type=MESH)

    @pl.when(core == 1)
    def _():
        for dx, dy in others:
            pl.semaphore_signal(barrier, inc=1, device_id=beyond(dx, dy), device_id_type=MESH)

    for d in range(1, CHIPS):
        @pl.when(z + d < CHIPS)
        def _():
            pl.semaphore_signal(barrier, inc=1, device_id=((seg + 2 * d) % NSEG, own), device_id_type=MESH)

    for load in load_i:
        load.wait()
    for s in range(NS):
        code[s] = sector_ref[0, s] * CHARGES + sector_ref[1, s]

    def sector_at(up, down):
        inside = (up >= 0) & (up < CHARGES) & (down >= 0) & (down < CHARGES)
        return inside, place[jnp.where(inside, up * CHARGES + down, 0)]

    def look_up(w, s):
        up, down = sector_ref[0, s], sector_ref[1, s]
        up_change, down_change = term_ref[0, w], term_ref[1, w]
        inside, found = sector_at(up - up_change, down - down_change)
        source[w * NS + s] = found
        mask[w * NS + s] = jnp.where(inside, live_ref[w].astype(F32), jnp.float32(0))
        target[w * NS + s] = sector_at(up + up_change, down + down_change)[1]

    load_w.wait()

    def add_square(t, total):
        found = jnp.int32(0)
        for s in range(NS):
            found = jnp.where(code[s] == t, jnp.int32(s), found)
        place[t] = found
        v = waves[0, t]
        return total + fold(v * v)

    def scale_from(squares):
        return lax.rsqrt(jnp.sum(squares) / ENTRIES + mean_eps)

    zero = jnp.zeros((8, BK), F32)
    squares = lax.fori_loop(0, NS, add_square, zero, unroll=2)
    scale = scale_from(squares)

    for w in range(SLOTS):
        load_l[w].wait()

        def set_left(s, carry):
            lcat[w, s] = beside(stage_l[w, s])
            look_up(w, s)
            return carry

        lax.fori_loop(0, NS, set_left, 0, unroll=2)

    def core_copy(src, dst, k):
        return pltpu.make_async_remote_copy(
            src_ref=src, dst_ref=dst, send_sem=core_send.at[k], recv_sem=core_recv.at[k],
            device_id=other_core, device_id_type=MESH,
        )

    def up_copy(src, dst, send, recv, d):
        return pltpu.make_async_remote_copy(
            src_ref=src, dst_ref=dst.at[d - 1], send_sem=send.at[d - 1], recv_sem=recv.at[d - 1],
            device_id=((seg + 2 * d) % NSEG, own), device_id_type=MESH,
        )

    def set_map(d, value):
        wdup[d - 1] = doubled(value)
        wt[d - 1] = beside(value.T)

    def first_maps():
        @pl.when(core == 1)
        def _():
            own_map = t_out[...]
            tdup[...] = doubled(own_map)
            tt[...] = beside(own_map.T)
            @pl.when(z < CHIPS - 1)
            def _():
                pl.semaphore_wait(ready, CHIPS - 1 - z)

            core_copy(t_out, t_in, 0).wait_recv()
            lower_map = t_in[...]
            set_map(1, lower_map)
            pair_out[...] = product(beside(lower_map), tdup[...])
            for d in range(1, CHIPS - 1):
                @pl.when((z >= 1) & (z + d < CHIPS))
                def _():
                    up_copy(pair_out, pair_in, pair_send, pair_recv, d).start()

    def more_maps(which):
        for d in which:
            @pl.when((core == 1) & (z >= d))
            def _():
                up_copy(pair_out, pair_in, pair_send, pair_recv, d - 1).wait_recv()
                set_map(d, product(beside(pair_in[d - 2]), wdup[d - 2]))

    def half(side):
        return pl.ds(side * HALF, HALF)

    def along(side, d):
        return at(0, d) if side == 0 else at(d, 0)

    def s1_copy(it, side, d, chunk):
        sector = chunk * SIDE + (y + d) % SIDE if side == 0 else ((x + d) % SIDE) * SIDE + chunk
        return pltpu.make_async_remote_copy(
            src_ref=image_parts.at[it, sector, half(side)], dst_ref=r1.at[it, side, d - 1, chunk],
            send_sem=s1_send.at[0], recv_sem=s1_recv.at[chunk],
            device_id=along(side, d), device_id_type=MESH,
        )

    def s2_copy(it, side, d, chunk, slot):
        return pltpu.make_async_remote_copy(
            src_ref=p2.at[it, side, chunk], dst_ref=r2.at[it, side, d - 1, slot],
            send_sem=s2_send.at[0], recv_sem=s2_recv.at[slot],
            device_id=along(1 - side, d), device_id_type=MESH,
        )

    def on_line(side, chunk):
        return chunk * SIDE + y if side == 0 else x * SIDE + chunk

    def gather_copy(it, side, d, chunk):
        block = images.at[it, on_line(side, chunk), half(side)]
        return pltpu.make_async_remote_copy(
            src_ref=block, dst_ref=block, send_sem=g_send.at[0], recv_sem=g_recv.at[chunk],
            device_id=along(side, d), device_id_type=MESH,
        )

    def wait_for(ref, sem):
        pltpu.make_async_copy(ref, ref, sem).wait()

    def small_copy(it, side, d):
        return pltpu.make_async_remote_copy(
            src_ref=small.at[it, side], dst_ref=small_in.at[it, side, d - 1],
            send_sem=small_send.at[side], recv_sem=small_recv.at[side],
            device_id=along(side, d), device_id_type=MESH,
        )

    def small_start(it, side, value):
        small[it, side] = value
        for d in (2, 1, 3):
            small_copy(it, side, d).start()

    def small_sum(it, side):
        wait_for(small_in.at[it, side], small_recv.at[side])
        return small[it, side] + small_in[it, side, 0] + small_in[it, side, 1] + small_in[it, side, 2]

    def small_end(it):
        for side in (0, 1):
            wait_for(small_in.at[it, side], small_send.at[side])

    def norm_copy(dx, dy):
        return pltpu.make_async_remote_copy(
            src_ref=norm_out, dst_ref=norm_in.at[dx * SIDE + dy - 1], send_sem=norm_send.at[0], recv_sem=norm_recv.at[0],
            device_id=at(dx, dy), device_id_type=MESH,
        )

    def lower_copy(dx, dy):
        return pltpu.make_async_remote_copy(
            src_ref=norm_out, dst_ref=lower_in.at[dx * SIDE + dy], send_sem=lower_send.at[0], recv_sem=lower_recv.at[0],
            device_id=beyond(dx, dy), device_id_type=MESH,
        )

    def left_half(t, v):
        left = jnp.concatenate([lcat[w, target[w * NS + t]] for w in range(SLOTS)], axis=0)
        high, low = split(product(left, doubled(v)))
        for w in range(SLOTS):
            part = slice(w * BK, (w + 1) * BK)
            inner[w, t] = jnp.concatenate([high[part], low[part]], axis=0)

    def right_half(s, scale):
        left = jnp.concatenate([inner[w, source[w * NS + s]] for w in range(SLOTS)], axis=1)
        both = lax.dot_general(left, rcat[s], (((1,), (1,)), ((), ())), preferred_element_type=F32)
        return (both[:BK, :BK] + both[:BK, BK:] + both[BK:, :BK] + both[BK:, BK:]) * scale

    for it in range(ITERS):
        if it == 0:
            def begin(t):
                v = waves[0, t] * scale
                waves[0, t] = v
                left_half(t, v)

            def set_right(s):
                for w in range(SLOTS):
                    high, low = split(stage_r[w, s] * mask[w * NS + s])
                    rcat[s, 0:BK, w * BK:(w + 1) * BK] = high
                    rcat[s, BK:2 * BK, w * BK:(w + 1) * BK] = low

            def begin_early(p, carry):
                begin(2 * p)
                begin(2 * p + 1)
                return carry

            def begin_late(p, carry):
                begin(EARLY + p)
                for j in range(NS // (NS - EARLY)):
                    set_right(NS // (NS - EARLY) * p + j)
                return carry

            lax.fori_loop(0, EARLY // 2, begin_early, 0)
            for load in load_r:
                load.wait()
            lax.fori_loop(0, NS - EARLY, begin_late, 0, unroll=2)
            scale = jnp.float32(1)

            load_t.wait()
            rows = lax.broadcasted_iota(jnp.int32, (BK, BK), 0)
            columns = lax.broadcasted_iota(jnp.int32, (BK, BK), 1)
            t_out[...] = stage_t[...] + jnp.where(rows == columns, jnp.float32(1), jnp.float32(0))
            pl.semaphore_wait(barrier, len(others) + 1 + z + (1 - core) * len(others))

            @pl.when(core == 0)
            def _():
                core_copy(t_out, t_in, 0).start()

            @pl.when(core == 1)
            def _():
                for d in range(1, CHIPS):
                    @pl.when(z >= d)
                    def _():
                        pl.semaphore_signal(
                            ready, inc=1, device_id=((seg - 2 * d + NSEG) % NSEG, own), device_id_type=MESH
                        )
        else:
            theta = jnp.sum(small_sum(it - 1, 1)) / ENTRIES

            squares = zero
            for chunk in range(SIDE):
                wait_for(r1.at[it - 1, :, :, chunk], g_recv.at[chunk])
                blocks = [sx * SIDE + sy for sx, sy in last_shell(chunk)]
                for t in blocks:
                    wave = waves[it - 1, t] * scale
                    wave = wave - step_size * (images[it - 1, t] - theta * wave)
                    left_half(t, wave)
                    waves[it, t] = wave
                    squares = squares + fold(wave * wave)
            scale = scale_from(squares)
            wait_for(r1.at[it - 1], g_send.at[0])
            small_end(it - 1)

        total = zero
        for chunk in range(SIDE):
            blocks = [sx * SIDE + sy for sx, sy in first_shell(chunk)]
            for s in blocks:
                block = right_half(s, scale)
                image_parts[it, s] = block
                total = total + fold(block * waves[it, s])
            for d in (2, 1, 3):
                for side in (0, 1):
                    s1_copy(it, side, d, chunk).start()
        small_start(it, 0, total * scale)
        if it == 0:
            first_maps()
        else:
            more_maps((3, 4) if it == 1 else (6, 7))

        for chunk in range(SIDE):
            wait_for(r1.at[it, :, :, chunk], s1_recv.at[chunk])
            for side in (0, 1):
                block = image_parts[it, on_line(side, chunk), half(side)]
                for e in range(SIDE - 1):
                    block = block + r1[it, side, e, chunk]
                p2[it, side, chunk] = block
                if it + 1 == ITERS:
                    d = (chunk - (x if side == 0 else y) + SIDE) % SIDE

                    @pl.when(d != 0)
                    def _():
                        s2_copy(it, side, d, chunk, 0).start()

            if it + 1 < ITERS:
                for d in (2, 1, 3):
                    for side in (0, 1):
                        s2_copy(it, side, d, chunk, chunk).start()


        def sum_of(side, chunk, slot):
            block = p2[it, side, chunk]
            for e in range(SIDE - 1):
                block = block + r2[it, side, e, slot]
            return block

        if it + 1 < ITERS:
            small_start(it, 1, small_sum(it, 0))
            for chunk in range(SIDE):
                wait_for(r2.at[it, :, :, chunk], s2_recv.at[chunk])
                for side in (0, 1):
                    images[it, on_line(side, chunk), half(side)] = sum_of(side, chunk, chunk)
                for d in (2, 1, 3):
                    for side in (0, 1):
                        gather_copy(it, side, d, chunk).start()
            wait_for(r2.at[it], s2_send.at[0])
            more_maps((2,) if it == 0 else (5,))
        else:
            small_start(it, 1, small_sum(it, 0))
            wait_for(r2.at[it, :, :, 0], s2_recv.at[0])
            image = jnp.concatenate([sum_of(0, x, 0), sum_of(1, y, 0)], axis=0)
            theta = jnp.sum(small_sum(it, 1)) / ENTRIES
            wave = waves[it, own] * scale
            wave = wave - step_size * (image - theta * wave)
            norm_out[...] = fold(wave * wave)
            for dx, dy in others:
                norm_copy(dx, dy).start()

            @pl.when(core == 0)
            def _():
                for dx, dy in others + [(0, 0)]:
                    lower_copy(dx, dy).start()

            wait_for(r2.at[it, :, :, 0], s2_send.at[0])
        wait_for(r1.at[it], s1_send.at[0])

    energy = product(beside(wave.T), doubled(image))

    @pl.when(core == 0)
    def _():
        e_out[...] = energy
        core_copy(e_out, e_in, 1).start()

    @pl.when(core == 1)
    def _():
        core_copy(e_out, e_in, 1).wait_recv()
        n_out[...] = product(tt[...], doubled(product(beside(e_in[...]), tdup[...])))

    squares = norm_out[...]
    wait_for(norm_in, norm_recv.at[0])
    for slot in range(NS - 1):
        squares = squares + norm_in[slot]
    scale = scale_from(squares)
    energy_scale = scale / BK

    out[0] = wave * scale

    @pl.when(core == 1)
    def _():
        wait_for(lower_in, lower_recv.at[0])
        lower_squares = lower_in[0]
        for slot in range(1, NS):
            lower_squares = lower_squares + lower_in[slot]
        lower = n_out[...] * (scale_from(lower_squares) / BK)
        f_out[...] = energy * energy_scale + lower
        for d in range(CHIPS - 1, 0, -1):
            @pl.when(z + d < CHIPS)
            def _():
                up_copy(f_out, f_in, f_send, f_recv, d).start()

        out[1] = lower
        n_out[...] = jnp.zeros((BK, BK), F32)
        for d in range(CHIPS - 1, 0, -1):
            @pl.when(z >= d)
            def _():
                up_copy(f_out, f_in, f_send, f_recv, d).wait_recv()
                n_out[...] += product(wt[d - 1], doubled(product(beside(f_in[d - 1]), wdup[d - 1])))

        core_copy(n_out, n_in, 2).start()
        out[1] += product(tt[...], doubled(product(beside(n_out[...]), tdup[...])))
        for d in range(1, CHIPS):
            @pl.when(z + d < CHIPS)
            def _():
                up_copy(f_out, f_in, f_send, f_recv, d).wait_send()

            if d < CHIPS - 1:
                @pl.when((z >= 1) & (z + d < CHIPS))
                def _():
                    up_copy(pair_out, pair_in, pair_send, pair_recv, d).wait_send()

        core_copy(n_out, n_in, 2).wait_send()

    @pl.when(core == 0)
    def _():
        core_copy(t_out, t_in, 0).wait_send()
        core_copy(e_out, e_in, 1).wait_send()
        wait_for(lower_in, lower_send.at[0])
        core_copy(n_out, n_in, 2).wait_recv()
        out[1] = n_in[...]

    wait_for(norm_in, norm_send.at[0])
    small_end(ITERS - 1)


def shards(wave_in, env_left, env_right, sector_charge, term_charge, term_live, transfer):
    vmem = pl.BlockSpec(memory_space=pltpu.VMEM)
    hbm = pl.BlockSpec(memory_space=pl.ANY)
    dma = pltpu.SemaphoreType.DMA
    square = pltpu.VMEM((BK, BK), F32)
    tile = pltpu.VMEM((8, BK), F32)
    both = pl.pallas_call(
        kernel,
        out_shape=jax.ShapeDtypeStruct((2, BK, BK), F32),
        in_specs=[hbm, hbm, hbm, hbm, hbm, hbm, hbm],
        out_specs=vmem,
        scratch_shapes=[
            pltpu.SMEM((2, NS), jnp.int32),
            pltpu.SMEM((2, SLOTS), jnp.int32),
            pltpu.SMEM((SLOTS,), jnp.int32),
            pltpu.SMEM((NS,), jnp.int32),
            pltpu.SMEM((NS,), jnp.int32),
            pltpu.SMEM((SLOTS * NS,), jnp.int32),
            pltpu.SMEM((SLOTS * NS,), jnp.int32),
            pltpu.SMEM((SLOTS * NS,), F32),
            pltpu.VMEM((SLOTS, NS, BK, BK), F32),
            pltpu.VMEM((SLOTS, NS, BK, BK), F32),
            square,
            pltpu.VMEM((SLOTS, NS, BK, 2 * BK), BF16),
            pltpu.VMEM((NS, 2 * BK, SLOTS * BK), BF16),
            pltpu.VMEM((SLOTS, NS, 2 * BK, BK), BF16),
            pltpu.VMEM((ITERS, NS, BK, BK), F32),
            pltpu.VMEM((ITERS, NS, BK, BK), F32),
            pltpu.VMEM((ITERS - 1, NS, BK, BK), F32),
            pltpu.VMEM((ITERS, 2, SIDE - 1, SIDE, HALF, BK), F32),
            pltpu.VMEM((ITERS, 2, SIDE, HALF, BK), F32),
            pltpu.VMEM((ITERS, 2, SIDE - 1, SIDE, HALF, BK), F32),
            pltpu.VMEM((ITERS, 2, 8, BK), F32),
            pltpu.VMEM((ITERS, 2, SIDE - 1, 8, BK), F32),
            tile,
            pltpu.VMEM((NS - 1, 8, BK), F32),
            square,
            square,
            square,
            pltpu.VMEM((CHIPS - 2, BK, BK), F32),
            pltpu.VMEM((2 * BK, 2 * BK), BF16),
            pltpu.VMEM((BK, 2 * BK), BF16),
            pltpu.VMEM((CHIPS - 1, 2 * BK, 2 * BK), BF16),
            pltpu.VMEM((CHIPS - 1, BK, 2 * BK), BF16),
            square,
            square,
            pltpu.VMEM((NS, 8, BK), F32),
            square,
            pltpu.VMEM((CHIPS - 1, BK, BK), F32),
            square,
            square,
            dma((5 + 2 * SLOTS,)),
            dma((1,)),
            dma((SIDE,)),
            dma((1,)),
            dma((SIDE,)),
            dma((1,)),
            dma((SIDE,)),
            dma((2,)),
            dma((2,)),
            dma((1,)),
            dma((1,)),
            dma((1,)),
            dma((1,)),
            pltpu.SemaphoreType.REGULAR,
            dma((3,)),
            dma((3,)),
            dma((CHIPS - 2,)),
            dma((CHIPS - 2,)),
            dma((CHIPS - 1,)),
            dma((CHIPS - 1,)),
        ],
        compiler_params=pltpu.CompilerParams(
            collective_id=0, has_side_effects=True, vmem_limit_bytes=56 * 1024 * 1024
        ),
    )(sector_charge.T, term_charge.T, term_live, wave_in, env_left, env_right, transfer)
    block = (1, 1, BK, BK)
    return both[0].reshape(block), both[1].reshape(block)


def solution(mesh):
    in_specs = (
        P("seg", None, None, None),
        P("seg", "term", None, None, None),
        P("seg", "term", None, None, None),
        P(),
        P("term", None),
        P("term"),
        P("seg", None, None, None),
    )
    out_specs = (P("seg", "term", None, None), P("seg", "term", None, None))
    return jax.shard_map(shards, mesh=mesh, in_specs=in_specs, out_specs=out_specs, check_vma=False)
```

```python
import functools

import jax
import jax.numpy as jnp
from jax import lax
from jax.experimental import pallas as pl
from jax.experimental.pallas import tpu as pltpu
from jax.sharding import PartitionSpec as P

ITERS = 3
SIDE = 4
CHARGES = 4
BK = 128
HALF = 64
NS = 16
SLOTS = 4
NSEG = 16
EARLY = 8
CHIPS = NSEG // 2
ENTRIES = float(NS * BK * BK)
mean_eps = 1e-06
step_size = 0.5

F32 = jnp.float32
BF16 = jnp.bfloat16
MESH = pl.DeviceIdType.MESH


def split(x):
    high = x.astype(BF16)
    low = (x - high.astype(F32)).astype(BF16)
    return high, low


def beside(x):
    return jnp.concatenate(split(x), axis=1)


def doubled(x):
    row = beside(x)
    return jnp.concatenate([row, row], axis=0)


def product(left, right):
    both = jnp.dot(left, right, preferred_element_type=F32)
    return both[:, :BK] + both[:, BK:]


def fold(x):
    return jnp.sum(x.reshape(x.shape[0] // 8, 8, x.shape[1]), axis=0)


def first_shell(r):
    return [(r, k) for k in range(r, SIDE)] + [(k, r) for k in range(r + 1, SIDE)]


def last_shell(r):
    return [(r, k) for k in range(r)] + [(k, r) for k in range(r)] + [(r, r)]


def kernel(
    sector_hbm, term_hbm, live_hbm, wave_hbm, left_hbm, right_hbm, transfer_hbm,
    out,
    sector_ref, term_ref, live_ref, code, place, source, target, mask,
    stage_l, stage_r, stage_t, lcat, rcat, inner, waves, image_parts, images,
    r1, p2, r2, small, small_in, norm_out, norm_in,
    t_out, t_in, pair_out, pair_in, tdup, tt, wdup, wt, e_out, e_in, lower_in, f_out, f_in, n_out, n_in,
    load_sem, s1_send, s1_recv, s2_send, s2_recv, g_send, g_recv,
    small_send, small_recv, norm_send, norm_recv, lower_send, lower_recv, ready, core_send, core_recv, pair_send, pair_recv, f_send, f_recv,
):
    seg = lax.axis_index("seg")
    own = lax.axis_index("term")
    x, y = own // SIDE, own % SIDE
    z, core = seg // 2, seg % 2

    def at(dx, dy):
        return (seg, ((x + dx) % SIDE) * SIDE + (y + dy) % SIDE)

    def beyond(dx, dy):
        return (seg + 1 - 2 * core, at(dx, dy)[1])

    other_core = beyond(0, 0)

    load_w = pltpu.make_async_copy(wave_hbm.at[0], waves.at[0], load_sem.at[0])
    load_t = pltpu.make_async_copy(transfer_hbm.at[0, own], stage_t, load_sem.at[1])
    load_i = [
        pltpu.make_async_copy(sector_hbm, sector_ref, load_sem.at[7]),
        pltpu.make_async_copy(term_hbm, term_ref, load_sem.at[8]),
        pltpu.make_async_copy(live_hbm, live_ref, load_sem.at[9]),
    ]
    for load in load_i:
        load.start()
    load_w.start()
    load_t.start()
    load_l = [pltpu.make_async_copy(left_hbm.at[0, w], stage_l.at[w], load_sem.at[2 + w]) for w in range(SLOTS)]
    load_r = pltpu.make_async_copy(right_hbm.at[0], stage_r, load_sem.at[6])
    for load in load_l + [load_r]:
        load.start()
    barrier = pltpu.get_barrier_semaphore()
    others = [(dx, dy) for dx in (2, 1, 3, 0) for dy in (2, 1, 3, 0) if (dx, dy) != (0, 0)]
    for dx, dy in others:
        pl.semaphore_signal(barrier, inc=1, device_id=at(dx, dy), device_id_type=MESH)
    pl.semaphore_signal(barrier, inc=1, device_id=other_core, device_id_type=MESH)

    @pl.when(core == 1)
    def _():
        for dx, dy in others:
            pl.semaphore_signal(barrier, inc=1, device_id=beyond(dx, dy), device_id_type=MESH)

    for d in range(1, CHIPS):
        @pl.when(z + d < CHIPS)
        def _():
            pl.semaphore_signal(barrier, inc=1, device_id=((seg + 2 * d) % NSEG, own), device_id_type=MESH)

    for load in load_i:
        load.wait()
    for s in range(NS):
        code[s] = sector_ref[0, s] * CHARGES + sector_ref[1, s]

    def sector_at(up, down):
        inside = (up >= 0) & (up < CHARGES) & (down >= 0) & (down < CHARGES)
        return inside, place[jnp.where(inside, up * CHARGES + down, 0)]

    def look_up(w, s):
        up, down = sector_ref[0, s], sector_ref[1, s]
        up_change, down_change = term_ref[0, w], term_ref[1, w]
        inside, found = sector_at(up - up_change, down - down_change)
        source[w * NS + s] = found
        mask[w * NS + s] = jnp.where(inside, live_ref[w].astype(F32), jnp.float32(0))
        target[w * NS + s] = sector_at(up + up_change, down + down_change)[1]

    load_w.wait()

    def add_square(t, total):
        found = jnp.int32(0)
        for s in range(NS):
            found = jnp.where(code[s] == t, jnp.int32(s), found)
        place[t] = found
        v = waves[0, t]
        return total + fold(v * v)

    def scale_from(squares):
        return lax.rsqrt(jnp.sum(squares) / ENTRIES + mean_eps)

    zero = jnp.zeros((8, BK), F32)
    squares = lax.fori_loop(0, NS, add_square, zero, unroll=2)
    scale = scale_from(squares)

    for w in range(SLOTS):
        load_l[w].wait()

        def set_left(s, carry):
            lcat[w, s] = beside(stage_l[w, s])
            look_up(w, s)
            return carry

        lax.fori_loop(0, NS, set_left, 0, unroll=2)

    def core_copy(src, dst, k):
        return pltpu.make_async_remote_copy(
            src_ref=src, dst_ref=dst, send_sem=core_send.at[k], recv_sem=core_recv.at[k],
            device_id=other_core, device_id_type=MESH,
        )

    def up_copy(src, dst, send, recv, d):
        return pltpu.make_async_remote_copy(
            src_ref=src, dst_ref=dst.at[d - 1], send_sem=send.at[d - 1], recv_sem=recv.at[d - 1],
            device_id=((seg + 2 * d) % NSEG, own), device_id_type=MESH,
        )

    def set_map(d, value):
        wdup[d - 1] = doubled(value)
        wt[d - 1] = beside(value.T)

    def first_maps():
        @pl.when(core == 1)
        def _():
            own_map = t_out[...]
            tdup[...] = doubled(own_map)
            tt[...] = beside(own_map.T)
            @pl.when(z < CHIPS - 1)
            def _():
                pl.semaphore_wait(ready, CHIPS - 1 - z)

            core_copy(t_out, t_in, 0).wait_recv()
            lower_map = t_in[...]
            set_map(1, lower_map)
            pair_out[...] = product(beside(lower_map), tdup[...])
            for d in range(1, CHIPS - 1):
                @pl.when((z >= 1) & (z + d < CHIPS))
                def _():
                    up_copy(pair_out, pair_in, pair_send, pair_recv, d).start()

    def more_maps(which):
        for d in which:
            @pl.when((core == 1) & (z >= d))
            def _():
                up_copy(pair_out, pair_in, pair_send, pair_recv, d - 1).wait_recv()
                set_map(d, product(beside(pair_in[d - 2]), wdup[d - 2]))

    def half(side):
        return pl.ds(side * HALF, HALF)

    def along(side, d):
        return at(0, d) if side == 0 else at(d, 0)

    def s1_copy(it, side, d, chunk):
        sector = chunk * SIDE + (y + d) % SIDE if side == 0 else ((x + d) % SIDE) * SIDE + chunk
        return pltpu.make_async_remote_copy(
            src_ref=image_parts.at[it, sector, half(side)], dst_ref=r1.at[it, side, d - 1, chunk],
            send_sem=s1_send.at[0], recv_sem=s1_recv.at[chunk],
            device_id=along(side, d), device_id_type=MESH,
        )

    def s2_copy(it, side, d, chunk, slot):
        return pltpu.make_async_remote_copy(
            src_ref=p2.at[it, side, chunk], dst_ref=r2.at[it, side, d - 1, slot],
            send_sem=s2_send.at[0], recv_sem=s2_recv.at[slot],
            device_id=along(1 - side, d), device_id_type=MESH,
        )

    def on_line(side, chunk):
        return chunk * SIDE + y if side == 0 else x * SIDE + chunk

    def gather_copy(it, side, d, chunk):
        block = images.at[it, on_line(side, chunk), half(side)]
        return pltpu.make_async_remote_copy(
            src_ref=block, dst_ref=block, send_sem=g_send.at[0], recv_sem=g_recv.at[chunk],
            device_id=along(side, d), device_id_type=MESH,
        )

    def wait_for(ref, sem):
        pltpu.make_async_copy(ref, ref, sem).wait()

    def small_copy(it, side, d):
        return pltpu.make_async_remote_copy(
            src_ref=small.at[it, side], dst_ref=small_in.at[it, side, d - 1],
            send_sem=small_send.at[side], recv_sem=small_recv.at[side],
            device_id=along(side, d), device_id_type=MESH,
        )

    def small_start(it, side, value):
        small[it, side] = value
        for d in (2, 1, 3):
            small_copy(it, side, d).start()

    def small_sum(it, side):
        wait_for(small_in.at[it, side], small_recv.at[side])
        return small[it, side] + small_in[it, side, 0] + small_in[it, side, 1] + small_in[it, side, 2]

    def small_end(it):
        for side in (0, 1):
            wait_for(small_in.at[it, side], small_send.at[side])

    def norm_copy(dx, dy):
        return pltpu.make_async_remote_copy(
            src_ref=norm_out, dst_ref=norm_in.at[dx * SIDE + dy - 1], send_sem=norm_send.at[0], recv_sem=norm_recv.at[0],
            device_id=at(dx, dy), device_id_type=MESH,
        )

    def lower_copy(dx, dy):
        return pltpu.make_async_remote_copy(
            src_ref=norm_out, dst_ref=lower_in.at[dx * SIDE + dy], send_sem=lower_send.at[0], recv_sem=lower_recv.at[0],
            device_id=beyond(dx, dy), device_id_type=MESH,
        )

    def left_half(t, v):
        left = jnp.concatenate([lcat[w, target[w * NS + t]] for w in range(SLOTS)], axis=0)
        high, low = split(product(left, doubled(v)))
        for w in range(SLOTS):
            part = slice(w * BK, (w + 1) * BK)
            inner[w, t] = jnp.concatenate([high[part], low[part]], axis=0)

    def right_half(s, scale):
        left = jnp.concatenate([inner[w, source[w * NS + s]] for w in range(SLOTS)], axis=1)
        both = lax.dot_general(left, rcat[s], (((1,), (1,)), ((), ())), preferred_element_type=F32)
        return (both[:BK, :BK] + both[:BK, BK:] + both[BK:, :BK] + both[BK:, BK:]) * scale

    for it in range(ITERS):
        if it == 0:
            def begin(t):
                v = waves[0, t] * scale
                waves[0, t] = v
                left_half(t, v)

            def set_right(s):
                for w in range(SLOTS):
                    high, low = split(stage_r[w, s] * mask[w * NS + s])
                    rcat[s, 0:BK, w * BK:(w + 1) * BK] = high
                    rcat[s, BK:2 * BK, w * BK:(w + 1) * BK] = low

            def begin_early(p, carry):
                begin(2 * p)
                begin(2 * p + 1)
                return carry

            def begin_late(p, carry):
                begin(EARLY + p)
                for j in range(NS // (NS - EARLY)):
                    set_right(NS // (NS - EARLY) * p + j)
                return carry

            lax.fori_loop(0, EARLY // 2, begin_early, 0)
            load_r.wait()
            lax.fori_loop(0, NS - EARLY, begin_late, 0, unroll=2)
            scale = jnp.float32(1)

            load_t.wait()
            rows = lax.broadcasted_iota(jnp.int32, (BK, BK), 0)
            columns = lax.broadcasted_iota(jnp.int32, (BK, BK), 1)
            t_out[...] = stage_t[...] + jnp.where(rows == columns, jnp.float32(1), jnp.float32(0))
            pl.semaphore_wait(barrier, len(others) + 1 + z + (1 - core) * len(others))

            @pl.when(core == 0)
            def _():
                core_copy(t_out, t_in, 0).start()

            @pl.when(core == 1)
            def _():
                for d in range(1, CHIPS):
                    @pl.when(z >= d)
                    def _():
                        pl.semaphore_signal(
                            ready, inc=1, device_id=((seg - 2 * d + NSEG) % NSEG, own), device_id_type=MESH
                        )
        else:
            theta = jnp.sum(small_sum(it - 1, 1)) / ENTRIES

            squares = zero
            for chunk in range(SIDE):
                wait_for(r1.at[it - 1, :, :, chunk], g_recv.at[chunk])
                blocks = [sx * SIDE + sy for sx, sy in last_shell(chunk)]
                for t in blocks:
                    wave = waves[it - 1, t] * scale
                    wave = wave - step_size * (images[it - 1, t] - theta * wave)
                    left_half(t, wave)
                    waves[it, t] = wave
                    squares = squares + fold(wave * wave)
            scale = scale_from(squares)
            wait_for(r1.at[it - 1], g_send.at[0])
            small_end(it - 1)

        total = zero
        for chunk in range(SIDE):
            blocks = [sx * SIDE + sy for sx, sy in first_shell(chunk)]
            for s in blocks:
                block = right_half(s, scale)
                image_parts[it, s] = block
                total = total + fold(block * waves[it, s])
            for d in (2, 1, 3):
                for side in (0, 1):
                    s1_copy(it, side, d, chunk).start()
        small_start(it, 0, total * scale)
        if it == 0:
            first_maps()
        else:
            more_maps((3, 4) if it == 1 else (6, 7))

        for chunk in range(SIDE):
            wait_for(r1.at[it, :, :, chunk], s1_recv.at[chunk])
            for side in (0, 1):
                block = image_parts[it, on_line(side, chunk), half(side)]
                for e in range(SIDE - 1):
                    block = block + r1[it, side, e, chunk]
                p2[it, side, chunk] = block
                if it + 1 == ITERS:
                    d = (chunk - (x if side == 0 else y) + SIDE) % SIDE

                    @pl.when(d != 0)
                    def _():
                        s2_copy(it, side, d, chunk, 0).start()

            if it + 1 < ITERS:
                for d in (2, 1, 3):
                    for side in (0, 1):
                        s2_copy(it, side, d, chunk, chunk).start()


        def sum_of(side, chunk, slot):
            block = p2[it, side, chunk]
            for e in range(SIDE - 1):
                block = block + r2[it, side, e, slot]
            return block

        if it + 1 < ITERS:
            small_start(it, 1, small_sum(it, 0))
            for chunk in range(SIDE):
                wait_for(r2.at[it, :, :, chunk], s2_recv.at[chunk])
                for side in (0, 1):
                    images[it, on_line(side, chunk), half(side)] = sum_of(side, chunk, chunk)
                for d in (2, 1, 3):
                    for side in (0, 1):
                        gather_copy(it, side, d, chunk).start()
            wait_for(r2.at[it], s2_send.at[0])
            more_maps((2,) if it == 0 else (5,))
        else:
            small_start(it, 1, small_sum(it, 0))
            wait_for(r2.at[it, :, :, 0], s2_recv.at[0])
            image = jnp.concatenate([sum_of(0, x, 0), sum_of(1, y, 0)], axis=0)
            theta = jnp.sum(small_sum(it, 1)) / ENTRIES
            wave = waves[it, own] * scale
            wave = wave - step_size * (image - theta * wave)
            norm_out[...] = fold(wave * wave)
            for dx, dy in others:
                norm_copy(dx, dy).start()

            @pl.when(core == 0)
            def _():
                for dx, dy in others + [(0, 0)]:
                    lower_copy(dx, dy).start()

        if it + 1 < ITERS:
            wait_for(r1.at[it], s1_send.at[0])

    energy = product(beside(wave.T), doubled(image))

    @pl.when(core == 0)
    def _():
        e_out[...] = energy
        core_copy(e_out, e_in, 1).start()

    @pl.when(core == 1)
    def _():
        core_copy(e_out, e_in, 1).wait_recv()
        n_out[...] = product(tt[...], doubled(product(beside(e_in[...]), tdup[...])))

    squares = norm_out[...]
    wait_for(norm_in, norm_recv.at[0])
    for slot in range(NS - 1):
        squares = squares + norm_in[slot]
    scale = scale_from(squares)
    energy_scale = scale / BK

    out[0] = wave * scale

    @pl.when(core == 1)
    def _():
        wait_for(lower_in, lower_recv.at[0])
        lower_squares = lower_in[0]
        for slot in range(1, NS):
            lower_squares = lower_squares + lower_in[slot]
        lower = n_out[...] * (scale_from(lower_squares) / BK)
        f_out[...] = energy * energy_scale + lower
        for d in (4, 5, 3, 6, 2, 7, 1):
            @pl.when(z + d < CHIPS)
            def _():
                up_copy(f_out, f_in, f_send, f_recv, d).start()

        out[1] = lower
        n_out[...] = jnp.zeros((BK, BK), F32)
        for d in (4, 5, 3, 6, 2, 7, 1):
            @pl.when(z >= d)
            def _():
                up_copy(f_out, f_in, f_send, f_recv, d).wait_recv()
                n_out[...] += product(wt[d - 1], doubled(product(beside(f_in[d - 1]), wdup[d - 1])))

        core_copy(n_out, n_in, 2).start()
        out[1] += product(tt[...], doubled(product(beside(n_out[...]), tdup[...])))
        for d in range(1, CHIPS):
            @pl.when(z + d < CHIPS)
            def _():
                up_copy(f_out, f_in, f_send, f_recv, d).wait_send()

            if d < CHIPS - 1:
                @pl.when((z >= 1) & (z + d < CHIPS))
                def _():
                    up_copy(pair_out, pair_in, pair_send, pair_recv, d).wait_send()

        core_copy(n_out, n_in, 2).wait_send()

    @pl.when(core == 0)
    def _():
        core_copy(t_out, t_in, 0).wait_send()
        core_copy(e_out, e_in, 1).wait_send()
        wait_for(lower_in, lower_send.at[0])
        core_copy(n_out, n_in, 2).wait_recv()
        out[1] = n_in[...]

    wait_for(norm_in, norm_send.at[0])
    wait_for(r2.at[ITERS - 1, :, :, 0], s2_send.at[0])
    wait_for(r1.at[ITERS - 1], s1_send.at[0])
    small_end(ITERS - 1)


def shards(wave_in, env_left, env_right, sector_charge, term_charge, term_live, transfer):
    vmem = pl.BlockSpec(memory_space=pltpu.VMEM)
    hbm = pl.BlockSpec(memory_space=pl.ANY)
    dma = pltpu.SemaphoreType.DMA
    square = pltpu.VMEM((BK, BK), F32)
    tile = pltpu.VMEM((8, BK), F32)
    both = pl.pallas_call(
        kernel,
        out_shape=jax.ShapeDtypeStruct((2, BK, BK), F32),
        in_specs=[hbm, hbm, hbm, hbm, hbm, hbm, hbm],
        out_specs=vmem,
        scratch_shapes=[
            pltpu.SMEM((2, NS), jnp.int32),
            pltpu.SMEM((2, SLOTS), jnp.int32),
            pltpu.SMEM((SLOTS,), jnp.int32),
            pltpu.SMEM((NS,), jnp.int32),
            pltpu.SMEM((NS,), jnp.int32),
            pltpu.SMEM((SLOTS * NS,), jnp.int32),
            pltpu.SMEM((SLOTS * NS,), jnp.int32),
            pltpu.SMEM((SLOTS * NS,), F32),
            pltpu.VMEM((SLOTS, NS, BK, BK), F32),
            pltpu.VMEM((SLOTS, NS, BK, BK), F32),
            square,
            pltpu.VMEM((SLOTS, NS, BK, 2 * BK), BF16),
            pltpu.VMEM((NS, 2 * BK, SLOTS * BK), BF16),
            pltpu.VMEM((SLOTS, NS, 2 * BK, BK), BF16),
            pltpu.VMEM((ITERS, NS, BK, BK), F32),
            pltpu.VMEM((ITERS, NS, BK, BK), F32),
            pltpu.VMEM((ITERS - 1, NS, BK, BK), F32),
            pltpu.VMEM((ITERS, 2, SIDE - 1, SIDE, HALF, BK), F32),
            pltpu.VMEM((ITERS, 2, SIDE, HALF, BK), F32),
            pltpu.VMEM((ITERS, 2, SIDE - 1, SIDE, HALF, BK), F32),
            pltpu.VMEM((ITERS, 2, 8, BK), F32),
            pltpu.VMEM((ITERS, 2, SIDE - 1, 8, BK), F32),
            tile,
            pltpu.VMEM((NS - 1, 8, BK), F32),
            square,
            square,
            square,
            pltpu.VMEM((CHIPS - 2, BK, BK), F32),
            pltpu.VMEM((2 * BK, 2 * BK), BF16),
            pltpu.VMEM((BK, 2 * BK), BF16),
            pltpu.VMEM((CHIPS - 1, 2 * BK, 2 * BK), BF16),
            pltpu.VMEM((CHIPS - 1, BK, 2 * BK), BF16),
            square,
            square,
            pltpu.VMEM((NS, 8, BK), F32),
            square,
            pltpu.VMEM((CHIPS - 1, BK, BK), F32),
            square,
            square,
            dma((6 + SLOTS,)),
            dma((1,)),
            dma((SIDE,)),
            dma((1,)),
            dma((SIDE,)),
            dma((1,)),
            dma((SIDE,)),
            dma((2,)),
            dma((2,)),
            dma((1,)),
            dma((1,)),
            dma((1,)),
            dma((1,)),
            pltpu.SemaphoreType.REGULAR,
            dma((3,)),
            dma((3,)),
            dma((CHIPS - 2,)),
            dma((CHIPS - 2,)),
            dma((CHIPS - 1,)),
            dma((CHIPS - 1,)),
        ],
        compiler_params=pltpu.CompilerParams(
            collective_id=0, has_side_effects=True, vmem_limit_bytes=56 * 1024 * 1024
        ),
    )(sector_charge.T, term_charge.T, term_live, wave_in, env_left, env_right, transfer)
    block = (1, 1, BK, BK)
    return both[0].reshape(block), both[1].reshape(block)


def solution(mesh):
    in_specs = (
        P("seg", None, None, None),
        P("seg", "term", None, None, None),
        P("seg", "term", None, None, None),
        P(),
        P("term", None),
        P("term"),
        P("seg", None, None, None),
    )
    out_specs = (P("seg", "term", None, None), P("seg", "term", None, None))
    return jax.shard_map(shards, mesh=mesh, in_specs=in_specs, out_specs=out_specs, check_vma=False)
```
